32 devices in a mesh: batch: 8 (over z, core), seq: 4 (over y, x).
Axes of the slice: x: 2, y: 2, z: 4, core: 2. Of those that a mesh axis runs over, the one named last changes fastest.
Arguments:
- tokens: bfloat16 [64, 1024, 1152], P('batch', 'seq'), may hold values from -6 to 6
- conditioning: bfloat16 [64, 4, 1152], P('batch'), may hold values from -6 to 6
- segments: int32 [64, 1024], P('batch', 'seq'), may hold values from 0 to 3, as said below
- kept: int32 [64, 512], P('batch', 'seq'), may hold values from 0 to 255, as said below
- cotangent: bfloat16 [64, 1024, 1152], P('batch', 'seq'), may hold values from -6 to 6
- mod_weight: bfloat16 [1152, 6912], P(('batch', 'seq')), may hold values from -0.1875 to 0.1875
- mod_bias: bfloat16 [6912], P(('batch', 'seq')), may hold values from -2 to 2
- qkv_weight: bfloat16 [1152, 3456], P(('batch', 'seq')), may hold values from -0.1875 to 0.1875
- query_bias: bfloat16 [1152], P(('batch', 'seq')), may hold values from -3 to 3
- value_bias: bfloat16 [1152], P(('batch', 'seq')), may hold values from -3 to 3
- out_weight: bfloat16 [1152, 1152], P(('batch', 'seq')), may hold values from -1.5 to 1.5
- out_bias: bfloat16 [1152], P(('batch', 'seq')), may hold values from -2 to 2
- up_weight: bfloat16 [1152, 4608], P(('batch', 'seq')), may hold values from -0.1875 to 0.1875
- up_bias: bfloat16 [4608], P(('batch', 'seq')), may hold values from -3 to 3
- down_weight: bfloat16 [4608, 1152], P(('batch', 'seq')), may hold values from -0.09375 to 0.09375
- down_bias: bfloat16 [1152], P(('batch', 'seq')), may hold values from -4 to 4
Outputs:
- output: bfloat16 [64, 1024, 1152], P('batch', 'seq')
- tokens_grad: bfloat16 [64, 1024, 1152], P('batch', 'seq')
- mod_weight_grad: float32 [1152, 6912], P(('batch', 'seq'))
- mod_bias_grad: float32 [6912], P(('batch', 'seq'))
- qkv_weight_grad: float32 [1152, 3456], P(('batch', 'seq'))
- query_bias_grad: float32 [1152], P(('batch', 'seq'))
- value_bias_grad: float32 [1152], P(('batch', 'seq'))
- out_weight_grad: float32 [1152, 1152], P(('batch', 'seq'))
- out_bias_grad: float32 [1152], P(('batch', 'seq'))
- up_weight_grad: float32 [1152, 4608], P(('batch', 'seq'))
- up_bias_grad: float32 [4608], P(('batch', 'seq'))
- down_weight_grad: float32 [4608, 1152], P(('batch', 'seq'))
- down_bias_grad: float32 [1152], P(('batch', 'seq'))
- sample_counts: int32 [64, 4, 2], P('batch')
The draws below stay inside these ranges and needn't reach their ends.
Inputs may be any that keep to these rules, and one draw needn't show every extreme that they name: `kept`: in each row, each aligned block of 128 entries lists, in increasing order, distinct positions among the 256 tokens of that row on one index of seq; positions 0 and 255 are always listed. `segments`: each row holds one of three packings: one sample of 1024 tokens, all numbered 0; 4 samples of 256 tokens numbered 0 to 3 in order; or a sample of 640 tokens numbered 0 followed by one of the remaining tokens numbered 1. In each aligned block of 8 rows at least one row is a single sample and at least one is of the third packing. Conditioning slots whose number a row does not use are read by nothing.
All inputs are finite; a program needn't handle non-finite values.
Results may differ from the reference program's by a relative error of at most 0.014.
The reference program's roundings to bfloat16 on the way count: a program that leaves them out, or rounds other values in their place, can miss the bound.
Values may be sent and summed in bfloat16 or wider, within the bound.
No kernel may reach another device: no remote copies, remote signals or barrier semaphores. Data moves between devices by JAX's collectives and lax.ppermute only.
A program may use at most 384 MiB of HBM per device.

```python
import jax
import jax.numpy as jnp
from jax import lax

D = 1152
HEADS = 16
HEAD_DIM = 72
FF = 4608
ROW_LEN = 1024
SEGS = 4
ROWS_DEV = 8
SEQ_TOK = 256
KEEP = 128
SMALL_LEN = 256
ROWS = 64
KEEP_ROW = 512
N_SEQ = 4


def draw_segments(key, part):
    key = jax.random.fold_in(key, 11)
    pick_key, toss_key = jax.random.split(key)
    groups = ROWS // ROWS_DEV
    chosen = jax.random.randint(pick_key, (groups, 1), 0, ROWS_DEV)
    kinds = jax.random.randint(toss_key, (groups, ROWS_DEV), 0, 3)
    slot_ids = jnp.arange(ROWS_DEV, dtype=jnp.int32)[None, :]
    kinds = jnp.where(slot_ids == chosen, 0, kinds)
    kinds = jnp.where(slot_ids == (chosen + 1) % ROWS_DEV, 2, kinds)
    kinds = kinds.reshape(ROWS, 1)
    places = jnp.arange(ROW_LEN, dtype=jnp.int32)[None, :]
    fourfold = places // SMALL_LEN
    twofold = (places >= ROW_LEN // 2 + SEQ_TOK // 2).astype(jnp.int32)
    picked = jnp.where(kinds == 1, fourfold, jnp.where(kinds == 2, twofold, 0))
    return picked.astype(jnp.int32)


def draw_kept(key, part):
    key = jax.random.fold_in(key, 23)
    piece_keys = jax.random.split(key, ROWS * N_SEQ)

    def one_piece(piece_key):
        order = jax.random.permutation(piece_key, SEQ_TOK - 2).astype(jnp.int32) + 1
        chosen = jnp.sort(order[:KEEP - 2])
        return jnp.concatenate([jnp.zeros((1,), jnp.int32), chosen, jnp.full((1,), SEQ_TOK - 1, jnp.int32)])
    return jax.vmap(one_piece)(piece_keys).reshape(ROWS, KEEP_ROW).astype(jnp.int32)


def with_spikes(values, own_key, source, target, blocks, factor):
    def block_of(axis_at):
        return (jnp.arange(values.shape[axis_at]) // (values.shape[axis_at] // blocks)).reshape((-1,) + (1,) * (values.ndim - 1 - axis_at))

    first = jax.random.permutation(own_key, blocks)[block_of(target)]
    far = (block_of(target) + blocks // 2) % blocks
    return jnp.where((block_of(source) == first) | (block_of(source) == far), factor * values, values)


def shard_levels(own_key, shape, cuts, least, top_value):
    def one(position, parts):
        draws = jax.random.uniform(jax.random.fold_in(jax.random.fold_in(own_key, 6), position), (parts,), jnp.float32, least / len(cuts), top_value / len(cuts))
        return jnp.repeat(jnp.exp(draws), shape[position] // parts).reshape((-1,) + (1,) * (len(shape) - position - 1))

    loudness = one(*cuts[0])
    for cut in cuts[1:]:
        loudness = loudness * one(*cut)
    return loudness


def gaussian(rng, shape, spread, most, pieces=(), kind=jnp.bfloat16):
    drawn = spread * jax.random.normal(rng, shape, jnp.float32)
    if pieces:
        drawn = drawn * shard_levels(rng, shape, pieces, -0.22, 0.18)
    return jnp.clip(drawn, -most, most).astype(kind)


def heavy_noise(key, extent, deviation, most, cuts, heavy, kind=jnp.bfloat16):
    drawn = deviation * jax.random.normal(key, extent, jnp.float32)
    if cuts:
        drawn = drawn * shard_levels(key, extent, cuts, -0.22, 0.18)
    return jnp.clip(with_spikes(drawn, jax.random.fold_in(key, 3), *heavy), -most, most).astype(kind)


def setup_inputs(seed: int = 0) -> dict:
    arg_keys = jax.random.split(jax.random.key(seed), 17)
    tokens = gaussian(arg_keys[0], (ROWS, ROW_LEN, D), 1.0, 6.0, ((0, 8), (1, 4)))
    conditioning = gaussian(arg_keys[1], (ROWS, SEGS, D), 1.0, 6.0, ((0, 8),))
    segments = draw_segments(jax.random.fold_in(arg_keys[16], 71), 0)
    kept = draw_kept(jax.random.fold_in(arg_keys[16], 71), 0)
    cotangent = heavy_noise(arg_keys[4], (ROWS, ROW_LEN, D), 1.0, 6.0, ((0, 8), (1, 4)), (0, 2, 8, 2.0))
    mod_weight = gaussian(arg_keys[5], (D, 6 * D), D ** -0.5, 0.1875, ((0, 32),))
    mod_bias = gaussian(arg_keys[6], (6 * D,), 0.3, 2.0, ((0, 32),))
    qkv_weight = gaussian(arg_keys[7], (D, 3 * D), D ** -0.5, 0.1875, ((0, 32),))
    query_bias = gaussian(arg_keys[8], (D,), 0.5, 3.0, ((0, 32),))
    value_bias = gaussian(arg_keys[9], (D,), 0.5, 3.0, ((0, 32),))
    out_weight = gaussian(arg_keys[10], (D, D), (D // 64) ** -0.5, 1.5, ((0, 32),))
    out_bias = gaussian(arg_keys[11], (D,), 0.3, 2.0, ((0, 32),))
    up_weight = gaussian(arg_keys[12], (D, FF), D ** -0.5, 0.1875, ((0, 32),))
    up_bias = gaussian(arg_keys[13], (FF,), 0.5, 3.0, ((0, 32),))
    down_weight = gaussian(arg_keys[14], (FF, D), FF ** -0.5, 0.09375, ((0, 32),))
    down_bias = gaussian(arg_keys[15], (D,), 0.8, 4.0, ((0, 32),))
    return {"tokens": tokens, "conditioning": conditioning, "segments": segments, "kept": kept, "cotangent": cotangent, "mod_weight": mod_weight, "mod_bias": mod_bias, "qkv_weight": qkv_weight, "query_bias": query_bias, "value_bias": value_bias, "out_weight": out_weight, "out_bias": out_bias, "up_weight": up_weight, "up_bias": up_bias, "down_weight": down_weight, "down_bias": down_bias}


HIGH = lax.Precision.HIGHEST
EPS = 1e-06
GELU_C = 0.7978845608028654
GELU_A = 0.044715

@jax.custom_vjp
def low(v):
    return lax.optimization_barrier(v.astype(jnp.bfloat16)).astype(jnp.float32)

@jax.custom_vjp
def low_back(v):
    return v

def low_keep(v):
    return (low(v), None)

def low_pass(kept, grad):
    return (grad,)

def back_keep(v):
    return (v, None)

def back_low(kept, grad):
    return (low(grad),)
low.defvjp(low_keep, low_pass)
low_back.defvjp(back_keep, back_low)

def both_ways(value):
    return low_back(low(value))

def matmul(left, right):
    return jnp.dot(left, right, precision=HIGH)

def normalize(values):
    center = values - lax.optimization_barrier(jnp.mean(values, -1, keepdims=True))
    return center * lax.rsqrt(lax.optimization_barrier(jnp.mean(center * center, -1, keepdims=True)) + EPS)

def row_layer(token_row, cond_row, seg_row, pos_row, param_set):
    mod_weight, mod_bias, qkv_weight, query_bias, value_bias, out_weight, out_bias, up_weight, up_bias, down_weight, down_bias = param_set
    inputs = token_row[pos_row]
    token_seg = seg_row[pos_row]
    cond_act = low(cond_row / (1.0 + jnp.exp(-cond_row)))
    modulation = matmul(cond_act, mod_weight) + mod_bias
    token_mod = modulation[token_seg]
    shift_one, scale_one, gate_one, shift_two, scale_two, gate_two = jnp.split(token_mod, 6, axis=-1)
    hidden_one = low(normalize(inputs) * (1.0 + scale_one) + shift_one)
    qkv = matmul(hidden_one, qkv_weight)
    queries = both_ways(qkv[:, :D] + query_bias)
    keys = both_ways(qkv[:, D:2 * D])
    values = both_ways(qkv[:, 2 * D:] + value_bias)
    query_heads = queries.reshape(KEEP_ROW, HEADS, HEAD_DIM)
    key_heads = keys.reshape(KEEP_ROW, HEADS, HEAD_DIM)
    value_heads = values.reshape(KEEP_ROW, HEADS, HEAD_DIM)
    scores = low_back(jnp.einsum('qhd,khd->hqk', query_heads, key_heads, precision=HIGH) * HEAD_DIM ** (-0.5))
    same = (token_seg[:, None] == token_seg[None, :])[None]
    scores = jnp.where(same, scores, -1e+30)
    top = lax.optimization_barrier(jnp.max(scores, -1, keepdims=True))
    expo = jnp.exp(scores - top)
    probs = expo / lax.optimization_barrier(jnp.sum(expo, -1, keepdims=True))
    attended = jnp.einsum('hqk,khd->qhd', low(probs), value_heads, precision=HIGH).reshape(KEEP_ROW, D)
    attended = both_ways(attended)
    branch_attn = low_back(matmul(attended, out_weight) + out_bias)
    mid = inputs + gate_one * branch_attn
    hidden_two = low(normalize(mid) * (1.0 + scale_two) + shift_two)
    pre_act = low_back(matmul(hidden_two, up_weight) + up_bias)
    activated = low(0.5 * pre_act * (1.0 + jnp.tanh(GELU_C * (pre_act + GELU_A * pre_act * pre_act * pre_act))))
    branch_mlp = low_back(matmul(activated, down_weight) + down_bias)
    result = mid + gate_two * branch_mlp
    return token_row.at[pos_row].set(result)

def reference(tokens, conditioning, segments, kept, cotangent, mod_weight, mod_bias, qkv_weight, query_bias, value_bias, out_weight, out_bias, up_weight, up_bias, down_weight, down_bias):
    weights = (mod_weight, mod_bias, qkv_weight, query_bias, value_bias, out_weight, out_bias, up_weight, up_bias, down_weight, down_bias)
    params = tuple((weight.astype(jnp.float32) for weight in weights))
    offsets = (jnp.arange(N_SEQ, dtype=jnp.int32) * SEQ_TOK)[None, :, None]
    positions = (kept.reshape(ROWS, N_SEQ, KEEP).astype(jnp.int32) + offsets).reshape(ROWS, KEEP_ROW).astype(jnp.int32)
    cond_all = conditioning.astype(jnp.float32)

    def forward(token_all, param_set):

        def one_row(row_items):
            token_row, cond_row, seg_row, pos_row = row_items
            return jax.checkpoint(row_layer)(token_row, cond_row, seg_row, pos_row, param_set)
        return lax.map(one_row, (token_all, cond_all, segments, positions))
    output, pullback = jax.vjp(forward, tokens.astype(jnp.float32), params)
    token_grad, param_grads = pullback(cotangent.astype(jnp.float32))
    token_seg = jnp.take_along_axis(segments, positions, 1)
    numbers = jnp.arange(SEGS, dtype=jnp.int32)
    kept_hits = lax.optimization_barrier(jnp.sum((token_seg[:, :, None] == numbers).astype(jnp.int32), 1))
    all_hits = lax.optimization_barrier(jnp.sum((segments[:, :, None] == numbers).astype(jnp.int32), 1))
    counts = jnp.stack([kept_hits, all_hits - kept_hits], -1).astype(jnp.int32)
    return (output.astype(jnp.bfloat16), token_grad.astype(jnp.bfloat16), param_grads[0], param_grads[1], param_grads[2], param_grads[3], param_grads[4], param_grads[5], param_grads[6], param_grads[7], param_grads[8], param_grads[9], param_grads[10], counts)
```

```python
import functools

import jax
import jax.numpy as jnp
from jax import lax
from jax.experimental import pallas as pl
from jax.experimental.pallas import tpu as pltpu
from jax.sharding import PartitionSpec as P

HEADS = 16
EPS = 1e-06
GELU_C = 0.7978845608028654
GELU_A = 0.044715
BF = jnp.bfloat16
F32 = jnp.float32
VMEM = 56 * 1024 * 1024


def normalize(values):
    center = values - jnp.mean(values, -1, keepdims=True)
    scale_inv = lax.rsqrt(jnp.mean(center * center, -1, keepdims=True) + EPS)
    return (center * scale_inv, scale_inv)


def norm_back(grad_norm, normed, scale_inv):
    return scale_inv * (
        grad_norm
        - jnp.mean(grad_norm, -1, keepdims=True)
        - normed * jnp.mean(grad_norm * normed, -1, keepdims=True)
    )


def dot_nn(a, b):
    return lax.dot_general(a, b, (((1,), (0,)), ((), ())), preferred_element_type=F32)


def dot_nt(a, b):
    return lax.dot_general(a, b, (((1,), (1,)), ((), ())), preferred_element_type=F32)


def dot_tn(a, b):
    return lax.dot_general(a, b, (((0,), (0,)), ((), ())), preferred_element_type=F32)


def attn_fwd_kernel(
    head_size, h_ref, qk_ref, vo_ref, qb_ref, vb_ref, ob_ref, segc_ref, segr_ref,
    q_out, k_out, v_out, att_out, lse_out, br_out,
):
    width = qb_ref.shape[-1]
    length = segr_ref.shape[-1]
    model = h_ref.shape[-1]
    h = h_ref[...].reshape(length, model)
    qk = dot_nt(h, qk_ref[0])
    v = (dot_nt(h, vo_ref[0, :width]) + vb_ref[0]).astype(BF)
    q = (qk[:, :width] + qb_ref[0]).astype(BF)
    k = qk[:, width:].astype(BF)
    part = q_out.shape[1:]
    q_out[0] = q.reshape(part)
    k_out[0] = k.reshape(part)
    v_out[0] = v.reshape(part)
    allowed = segc_ref[0] == segr_ref[0]
    scale = head_size ** (-0.5)
    pieces = []
    for i in range(width // head_size):
        cut = slice(i * head_size, (i + 1) * head_size)
        score = jnp.where(allowed, dot_nt(k[:, cut], q[:, cut]) * scale, -1e30)
        top = jnp.max(score, 0, keepdims=True)
        prob = jnp.exp(score - top)
        total = jnp.sum(prob, 0, keepdims=True)
        out_t = dot_tn(v[:, cut], prob.astype(BF)) * (1.0 / total)
        pieces.append(out_t.T)
        lse_out[0, 0, i : i + 1, :] = top + jnp.log(total)
    att = jnp.concatenate(pieces, -1).astype(BF)
    att_out[0] = att.reshape(part)
    term = dot_nn(att, vo_ref[0, width:])

    @pl.when(pl.program_id(1) == 0)
    def _():
        br_out[...] = (term + ob_ref[...]).reshape(br_out.shape)

    @pl.when(pl.program_id(1) != 0)
    def _():
        br_out[...] += term.reshape(br_out.shape)


def attn_bwd_kernel(
    head_size, h_ref, gb_ref, qk_ref, vo_ref, q_ref, k_ref, v_ref, att_ref, lse_ref, segc_ref, segr_ref,
    gqk_out, gvo_out, gh_out, gqb_out, gvb_out, sum_qkv, sum_out,
):
    width = q_ref.shape[-1]
    length = segr_ref.shape[-1]
    model = h_ref.shape[-1]
    block, row = pl.program_id(0), pl.program_id(1)
    h = h_ref[:, pl.ds(row, 1)].reshape(length, model)
    gb = gb_ref[:, pl.ds(row, 1)].reshape(length, model)
    grad_att = dot_nt(gb, vo_ref[0, width:]).astype(BF)
    q = q_ref[...].reshape(length, width)
    k = k_ref[...].reshape(length, width)
    v = v_ref[...].reshape(length, width)
    att = att_ref[...].reshape(length, width)
    allowed = segc_ref[0] == segr_ref[0]
    scale = head_size ** (-0.5)
    gq, gk, gv = [], [], []
    for i in range(width // head_size):
        cut = slice(i * head_size, (i + 1) * head_size)
        score = dot_nt(k[:, cut], q[:, cut]) * scale - lse_ref[0, 0, i : i + 1, :]
        prob = jnp.exp(jnp.where(allowed, score, -1e30))
        grad_prob = dot_nt(v[:, cut], grad_att[:, cut])
        inner = jnp.sum(prob * grad_prob, 0, keepdims=True)
        grad_score = (prob * (grad_prob - inner)).astype(BF)
        gq.append((dot_tn(k[:, cut], grad_score) * scale).T)
        gk.append(dot_nn(grad_score, q[:, cut]) * scale)
        gv.append(dot_nn(prob.astype(BF), grad_att[:, cut]))
    gq, gk, gv = [jnp.concatenate(p, -1).astype(BF) for p in (gq, gk, gv)]
    grad_qkv = jnp.concatenate([gq, gk, gv], -1)
    weights = jnp.concatenate([qk_ref[0], vo_ref[0, :width]], 0)
    term = dot_nn(grad_qkv, weights).reshape(gh_out.shape[0], 1, gh_out.shape[2], model)
    term_qkv = dot_tn(grad_qkv, h)
    term_out = dot_tn(att, gb)
    qb_sum = jnp.sum(gq.astype(F32), 0, keepdims=True)
    vb_sum = jnp.sum(gv.astype(F32), 0, keepdims=True)

    @pl.when(block == 0)
    def _():
        gh_out[:, pl.ds(row, 1)] = term

    @pl.when(block != 0)
    def _():
        gh_out[:, pl.ds(row, 1)] += term

    @pl.when(row == 0)
    def _():
        sum_qkv[...] = term_qkv
        sum_out[...] = term_out
        gqb_out[0] = qb_sum
        gvb_out[0] = vb_sum

    @pl.when(row != 0)
    def _():
        sum_qkv[...] += term_qkv
        sum_out[...] += term_out
        gqb_out[0] += qb_sum
        gvb_out[0] += vb_sum

    @pl.when(row == pl.num_programs(1) - 1)
    def _():
        gqk_out[0] = sum_qkv[: 2 * width].astype(BF)
        gvo_out[0, :width] = sum_qkv[2 * width :].astype(BF)
        gvo_out[0, width:] = sum_out[...].astype(BF)


def attn_fwd(hidden, qk_w, vo_w, query_bias, value_bias, out_bias, seg_col, seg_row, head_size):
    n_seq, rows, kept_count, model = hidden.shape
    blocks, _, width = query_bias.shape
    length = n_seq * kept_count
    heads = width // head_size
    token = pl.BlockSpec((n_seq, 1, kept_count, model), lambda r, e: (0, r, 0, 0))
    part = pl.BlockSpec((1, n_seq, 1, kept_count, width), lambda r, e: (e, 0, r, 0, 0))
    weight = pl.BlockSpec((1, 2 * width, model), lambda r, e: (e, 0, 0))
    bias = pl.BlockSpec((1, 1, width), lambda r, e: (e, 0, 0))
    part_shape = jax.ShapeDtypeStruct((blocks, n_seq, rows, kept_count, width), BF)
    return pl.pallas_call(
        functools.partial(attn_fwd_kernel, head_size),
        grid=(rows, blocks),
        in_specs=[
            token, weight, weight, bias, bias,
            pl.BlockSpec((1, model), lambda r, e: (0, 0)),
            pl.BlockSpec((1, length, 1), lambda r, e: (r, 0, 0)),
            pl.BlockSpec((1, 1, length), lambda r, e: (r, 0, 0)),
        ],
        out_specs=[
            part, part, part, part,
            pl.BlockSpec((1, 1, heads, length), lambda r, e: (e, r, 0, 0)),
            token,
        ],
        out_shape=[
            part_shape, part_shape, part_shape, part_shape,
            jax.ShapeDtypeStruct((blocks, rows, heads, length), F32),
            jax.ShapeDtypeStruct(hidden.shape, F32),
        ],
        compiler_params=pltpu.CompilerParams(vmem_limit_bytes=VMEM),
        cost_estimate=pl.CostEstimate(
            flops=2 * rows * length * model * width * blocks * 6, bytes_accessed=40 << 20, transcendentals=0
        ),
    )(hidden, qk_w, vo_w, query_bias, value_bias, out_bias, seg_col, seg_row)


def attn_bwd(hidden, grad_branch, qk_w, vo_w, q, k, v, att, lse, seg_col, seg_row, head_size):
    n_seq, rows, kept_count, model = hidden.shape
    blocks, width = q.shape[0], q.shape[-1]
    length = n_seq * kept_count
    heads = width // head_size
    whole = pl.BlockSpec(hidden.shape, lambda e, r: (0, 0, 0, 0))
    part = pl.BlockSpec((1, n_seq, 1, kept_count, width), lambda e, r: (e, 0, r, 0, 0))
    weight = pl.BlockSpec((1, 2 * width, model), lambda e, r: (e, 0, 0))
    bias = pl.BlockSpec((1, 1, width), lambda e, r: (e, 0, 0))
    return pl.pallas_call(
        functools.partial(attn_bwd_kernel, head_size),
        grid=(blocks, rows),
        in_specs=[
            whole, whole, weight, weight, part, part, part, part,
            pl.BlockSpec((1, 1, heads, length), lambda e, r: (e, r, 0, 0)),
            pl.BlockSpec((1, length, 1), lambda e, r: (r, 0, 0)),
            pl.BlockSpec((1, 1, length), lambda e, r: (r, 0, 0)),
        ],
        out_specs=[weight, weight, whole, bias, bias],
        out_shape=[
            jax.ShapeDtypeStruct(qk_w.shape, BF),
            jax.ShapeDtypeStruct(vo_w.shape, BF),
            jax.ShapeDtypeStruct(hidden.shape, F32),
            jax.ShapeDtypeStruct((blocks, 1, width), F32),
            jax.ShapeDtypeStruct((blocks, 1, width), F32),
        ],
        scratch_shapes=[pltpu.VMEM((3 * width, model), F32), pltpu.VMEM((width, model), F32)],
        compiler_params=pltpu.CompilerParams(vmem_limit_bytes=VMEM),
        cost_estimate=pl.CostEstimate(
            flops=2 * rows * length * model * width * blocks * 14, bytes_accessed=40 << 20, transcendentals=0
        ),
    )(hidden, grad_branch, qk_w, vo_w, q, k, v, att, lse, seg_col, seg_row)


def body(
    n_batch, n_seq,
    tokens, conditioning, segments, kept, cotangent,
    mod_weight, mod_bias, qkv_weight, query_bias, value_bias, out_weight, out_bias,
    up_weight, up_bias, down_weight, down_bias,
):
    row_count, seq_tokens, model = tokens.shape
    kept_count = kept.shape[1]
    slots = conditioning.shape[1]
    head_size = model // HEADS
    rows = row_count // n_seq
    shard = qkv_weight.shape[0]
    n_z = n_batch // 2
    blocks = 2 * n_seq
    width = model // blocks
    flat = n_seq * rows * kept_count
    ff_shard = down_weight.shape[0]
    batch_at = lax.axis_index("batch")
    seq_at = lax.axis_index("seq")
    core_at = batch_at % 2
    block_at = core_at * n_seq + seq_at
    relative = block_at ^ jnp.arange(blocks)
    seq_relative = seq_at ^ jnp.arange(n_seq)
    bits = [1 << i for i in range(n_seq.bit_length() - 1)]
    z_groups = [[2 * z + c for z in range(n_z)] for c in range(2)]

    def over_core(value):
        return lax.ppermute(value, "batch", [(i, i ^ 1) for i in range(n_batch)])

    def over_seq(value, by):
        return lax.ppermute(value, "seq", [(i, i ^ by) for i in range(n_seq)])

    def over_block(value, by):
        moves = []
        for b in range(n_batch):
            for s in range(n_seq):
                to = (b ^ (by // n_seq)) * n_seq + (s ^ (by % n_seq))
                moves.append((b * n_seq + s, to))
        return lax.ppermute(value, ("batch", "seq"), moves)

    def exchange_blocks(value):
        mine = jnp.take(value, relative, axis=0)
        got = [mine[0]] + [over_block(mine[j], j) for j in range(1, blocks)]
        return jnp.take(jnp.stack(got), relative, axis=0)

    def gather_z(value):
        return lax.all_gather(value, "batch", axis=0, tiled=True, axis_index_groups=z_groups)

    def scatter_z(value):
        return lax.psum_scatter(value, "batch", scatter_dimension=0, tiled=True, axis_index_groups=z_groups)

    def gather_blocks(own, order):
        held = {0: own}
        for bit in order:
            for j in list(held):
                held[j | bit] = over_seq(held[j], bit)
        for j in list(held):
            held[j | n_seq] = over_core(held[j])
        return jnp.stack([held[j] for j in range(blocks)])

    def scatter_blocks(value, order):
        held = {j: value[j] for j in range(blocks)}

        def fold(bit, send):
            for j in [j for j in held if j & bit]:
                got = send(held.pop(j))
                held[j ^ bit] = (held[j ^ bit].astype(F32) + got.astype(F32)).astype(BF)

        fold(n_seq, over_core)
        for bit in order:
            fold(bit, lambda v, bit=bit: over_seq(v, bit))
        return held[0]

    def to_rows(value):
        got = [lax.dynamic_slice_in_dim(value, seq_at * rows, rows, 0)]
        for j in range(1, n_seq):
            got.append(over_seq(lax.dynamic_slice_in_dim(value, (seq_at ^ j) * rows, rows, 0), j))
        return jnp.stack(got)

    def from_rows(value):
        got = [value[0]] + [over_seq(value[j], j) for j in range(1, n_seq)]
        return jnp.take(jnp.stack(got), seq_relative, axis=0).reshape((row_count,) + value.shape[2:])

    places = jnp.arange(seq_tokens, dtype=jnp.int32)
    pick = (kept[:, :, None] == places).astype(BF)
    kept_here = jnp.any(kept[:, :, None] == places, 1)

    def pick_kept(value):
        return jnp.einsum("rkt,rtd->rkd", pick, value, preferred_element_type=F32).astype(BF)

    def put_kept(value, base):
        spread = jnp.einsum("rkt,rkd->rtd", pick, value, preferred_element_type=F32).astype(BF)
        return jnp.where(kept_here[:, :, None], spread, base)

    inputs = to_rows(pick_kept(tokens)).reshape(flat, model).astype(F32)

    qkv_cols = qkv_weight.reshape(shard, 3, blocks, width).transpose(2, 0, 1, 3).reshape(blocks, shard, 3 * width)
    qkv_own = gather_z(exchange_blocks(qkv_cols).reshape(blocks * shard, 3 * width)).T
    spread_out = [(d, ((d // n_z) // n_seq + 2 * (d % n_z)) * n_seq + (d // n_z) % n_seq) for d in range(n_batch * n_seq)]
    out_own = gather_z(lax.ppermute(out_weight, ("batch", "seq"), spread_out))
    qk_w = gather_blocks(qkv_own[: 2 * width], bits)
    vo_w = gather_blocks(jnp.concatenate([qkv_own[2 * width :], out_own]), bits[::-1])
    up_cols = up_weight.reshape(shard, n_z, blocks, ff_shard).transpose(2, 0, 1, 3).reshape(blocks, shard, n_z * ff_shard)
    up_own = gather_z(exchange_blocks(up_cols).reshape(blocks * shard, n_z * ff_shard)).T
    down_own = gather_z(down_weight)
    up_w = gather_blocks(up_own, bits).reshape(-1, model)
    down_w = gather_blocks(down_own, bits[::-1]).reshape(-1, model)

    packed = jnp.concatenate([mod_bias, query_bias, value_bias, out_bias, up_bias, down_bias])
    packed = lax.all_gather(packed, ("batch", "seq"), axis=0).astype(F32)
    cuts = [0]
    for item in (mod_bias, query_bias, value_bias, out_bias, up_bias, down_bias):
        cuts.append(cuts[-1] + item.shape[0])
    mod_b, query_b, value_b, out_b, up_b, down_b = [
        packed[:, cuts[i] : cuts[i + 1]].reshape(-1) for i in range(6)
    ]
    query_b = jnp.take(query_b.reshape(blocks, 1, width), relative, axis=0)
    value_b = jnp.take(value_b.reshape(blocks, 1, width), relative, axis=0)
    up_b = jnp.take(
        up_b.reshape(n_z, blocks, ff_shard).transpose(1, 0, 2).reshape(blocks, -1), relative, axis=0
    ).reshape(1, -1)

    numbers = jnp.arange(slots, dtype=jnp.int32)
    query_seg = jnp.take_along_axis(segments, kept, axis=1)
    kept_hits = jnp.sum((query_seg[:, :, None] == numbers).astype(jnp.int32), 1)
    all_hits = jnp.sum((segments[:, :, None] == numbers).astype(jnp.int32), 1)
    small = jnp.concatenate([query_seg, kept_hits, all_hits - kept_hits], -1)
    small = lax.all_gather(small, "seq", axis=0)
    sample_counts = jnp.sum(small[:, :, kept_count:], 0).reshape(row_count, 2, slots).transpose(0, 2, 1)
    seg = lax.dynamic_slice_in_dim(small[:, :, :kept_count], seq_at * rows, rows, 1)
    seg = jnp.take(seg, seq_relative, axis=0)
    seg_rows = seg.transpose(1, 0, 2).reshape(rows, 1, n_seq * kept_count)
    seg_cols = seg_rows.reshape(rows, n_seq * kept_count, 1)

    cond_float = conditioning.astype(F32)
    cond_act = (cond_float / (1.0 + jnp.exp(-cond_float))).astype(BF)
    act_all = lax.all_gather(cond_act, "batch", axis=0)
    act_mine = lax.dynamic_slice_in_dim(act_all, seq_at * rows, rows, 1).reshape(-1, model)
    act_cols = lax.dynamic_slice_in_dim(act_mine, batch_at * n_seq * shard, n_seq * shard, 1)
    mod_rows = lax.all_gather(mod_weight, "seq", axis=0, tiled=True)
    mod_part = jnp.dot(act_cols, mod_rows, preferred_element_type=F32)
    modulation = lax.psum_scatter(mod_part, "batch", scatter_dimension=0, tiled=True) + mod_b
    modulation = modulation.reshape(rows, slots, 6, model)

    hit = seg[:, :, :, None, None] == numbers[:, None]

    def token_mod(index):
        table = modulation[:, :, index]
        value = table[None, :, None, 0]
        for slot in range(1, slots):
            value = jnp.where(seg[:, :, :, None] == slot, table[None, :, None, slot], value)
        return value.reshape(flat, model)

    def slot_sums(value):
        split = value.reshape(n_seq, rows, kept_count, model)
        sums = [jnp.sum(jnp.where(seg[:, :, :, None] == slot, split, 0.0), (0, 2)) for slot in range(slots)]
        return jnp.stack(sums, 1)

    normed_one, inv_one = normalize(inputs)
    hidden_one = (normed_one * (1.0 + token_mod(1)) + token_mod(0)).astype(BF)
    hidden_one = hidden_one.reshape(n_seq, rows, kept_count, model)
    q, k, v, att, lse, branch_attn = attn_fwd(
        hidden_one, qk_w, vo_w, query_b, value_b, out_b.reshape(1, -1), seg_cols, seg_rows, head_size
    )
    branch_attn = branch_attn.reshape(flat, model)
    mid = inputs + token_mod(2) * branch_attn
    normed_two, inv_two = normalize(mid)
    hidden_two = (normed_two * (1.0 + token_mod(4)) + token_mod(3)).astype(BF)

    grad_result = to_rows(pick_kept(cotangent)).reshape(flat, model).astype(F32)
    grad_mlp = (grad_result * token_mod(5)).astype(BF)

    pre = dot_nt(hidden_two, up_w) + up_b
    tanh_part = jnp.tanh(GELU_C * (pre + GELU_A * pre * pre * pre))
    activated = (0.5 * pre * (1.0 + tanh_part)).astype(BF)
    slope = 0.5 * (1.0 + tanh_part) + 0.5 * pre * (1.0 - tanh_part * tanh_part) * GELU_C * (
        1.0 + 3.0 * GELU_A * pre * pre
    )
    branch_mlp = dot_nn(activated, down_w) + down_b
    grad_pre = (dot_nt(grad_mlp, down_w) * slope).astype(BF)
    grad_down = dot_tn(activated, grad_mlp).astype(BF).reshape(blocks, -1, model)
    grad_up = dot_tn(grad_pre, hidden_two).astype(BF).reshape(blocks, -1, model)
    grad_hidden_two = dot_nn(grad_pre, up_w)
    grad_up_bias = jnp.sum(grad_pre.astype(F32), 0)
    grad_down_bias = jnp.sum(grad_mlp.astype(F32), 0)

    result = (mid + token_mod(5) * branch_mlp).astype(BF).reshape(n_seq, rows, kept_count, model)
    output = put_kept(from_rows(result), tokens)

    down_sum = scatter_z(scatter_blocks(grad_down, bits))
    up_sum = scatter_z(scatter_blocks(grad_up, bits[::-1]).T)

    grad_mid = grad_result + norm_back(grad_hidden_two * (1.0 + token_mod(4)), normed_two, inv_two)
    grad_branch = (grad_mid * token_mod(2)).astype(BF)
    grad_out_bias = jnp.sum(grad_branch.astype(F32), 0)
    grad_qk, grad_vo, grad_hidden_one, grad_query_bias, grad_value_bias = attn_bwd(
        hidden_one, grad_branch.reshape(hidden_one.shape), qk_w, vo_w, q, k, v, att, lse, seg_cols, seg_rows, head_size
    )
    grad_hidden_one = grad_hidden_one.reshape(flat, model)
    grad_inputs = grad_mid + norm_back(grad_hidden_one * (1.0 + token_mod(1)), normed_one, inv_one)
    grad_inputs = grad_inputs.astype(BF).reshape(n_seq, rows, kept_count, model)
    tokens_grad = put_kept(from_rows(grad_inputs), cotangent)

    qk_sum = scatter_blocks(grad_qk, bits)
    vo_sum = scatter_blocks(grad_vo, bits[::-1])
    qkv_sum = scatter_z(jnp.concatenate([qk_sum, vo_sum[:width]]).T)
    out_sum = scatter_z(vo_sum[width:])

    def columns(value, parts):
        value = exchange_blocks(value.reshape(blocks, shard, -1)).reshape(blocks, shard, parts, -1)
        return value.transpose(1, 2, 0, 3).reshape(shard, -1).astype(F32)

    qkv_grad = columns(qkv_sum, 3)
    up_grad = columns(up_sum, n_z)
    out_grad = lax.ppermute(out_sum, ("batch", "seq"), [(t, d) for d, t in spread_out]).astype(F32)
    down_grad = down_sum.astype(F32)

    pieces = [
        slot_sums(grad_hidden_one),
        slot_sums(grad_hidden_one * normed_one),
        slot_sums(grad_mid * branch_attn),
        slot_sums(grad_hidden_two),
        slot_sums(grad_hidden_two * normed_two),
        slot_sums(grad_result * branch_mlp),
    ]
    grad_mod = jnp.concatenate(pieces, -1).reshape(rows * slots, 6 * model).astype(BF)
    grad_mod = lax.all_gather(grad_mod, ("batch", "seq"), axis=0, tiled=True)
    device_at = batch_at * n_seq + seq_at
    act_own = lax.dynamic_slice_in_dim(act_all.reshape(-1, model), device_at * shard, shard, 1)
    mod_grad = dot_tn(act_own, grad_mod)
    mod_bias_grad = lax.dynamic_slice_in_dim(jnp.sum(grad_mod.astype(F32), 0), device_at * mod_bias.shape[0], mod_bias.shape[0])

    def natural(value):
        return jnp.take(value.reshape(blocks, -1), relative, axis=0)

    natural_up = natural(grad_up_bias).reshape(blocks, n_z, ff_shard).transpose(1, 0, 2)
    shares = [
        value.reshape(n_batch * n_seq, -1)
        for value in (natural(grad_query_bias), natural(grad_value_bias), grad_out_bias, natural_up, grad_down_bias)
    ]
    bias_sum = lax.psum_scatter(jnp.concatenate(shares, -1), ("batch", "seq"), scatter_dimension=0, tiled=True)[0]
    bias_grads = []
    at = 0
    for share in shares:
        bias_grads.append(lax.slice_in_dim(bias_sum, at, at + share.shape[1]))
        at += share.shape[1]
    return (
        output, tokens_grad, mod_grad, mod_bias_grad, qkv_grad, bias_grads[0], bias_grads[1],
        out_grad, bias_grads[2], up_grad, bias_grads[3], down_grad, bias_grads[4], sample_counts,
    )


def solution(mesh):
    both = ("batch", "seq")
    row_split = P("batch", "seq", None)
    matrix = P(both, None)
    vector = P(both)
    return jax.shard_map(
        functools.partial(body, mesh.shape["batch"], mesh.shape["seq"]),
        mesh=mesh,
        in_specs=(
            row_split, P("batch", None, None), P("batch", "seq"), P("batch", "seq"), row_split,
            matrix, vector, matrix, vector, vector, matrix, vector, matrix, vector, matrix, vector,
        ),
        out_specs=(
            row_split, row_split, matrix, vector, matrix, vector, vector,
            matrix, vector, matrix, vector, matrix, vector, P("batch", None, None),
        ),
        check_vma=False,
    )
```

```python
import functools

import jax
import jax.numpy as jnp
from jax import lax
from jax.experimental import pallas as pl
from jax.experimental.pallas import tpu as pltpu
from jax.sharding import Mesh
from jax.sharding import PartitionSpec as P

HEADS = 16
EPS = 1e-06
GELU_C = 0.7978845608028654
GELU_A = 0.044715
BF = jnp.bfloat16
F32 = jnp.float32
VMEM = 58 * 1024 * 1024
ANY = pl.BlockSpec(memory_space=pl.ANY)
EVERY = ("z", "core", "seq")
DENSE = ("core", "seq")


def normalize(values):
    center = values - jnp.mean(values, -1, keepdims=True)
    scale_inv = lax.rsqrt(jnp.mean(center * center, -1, keepdims=True) + EPS)
    return (center * scale_inv, scale_inv)


def norm_back(grad_norm, normed, scale_inv):
    return scale_inv * (
        grad_norm
        - jnp.mean(grad_norm, -1, keepdims=True)
        - normed * jnp.mean(grad_norm * normed, -1, keepdims=True)
    )


def dot_nn(a, b):
    return lax.dot_general(a, b, (((1,), (0,)), ((), ())), preferred_element_type=F32)


def dot_nt(a, b):
    return lax.dot_general(a, b, (((1,), (1,)), ((), ())), preferred_element_type=F32)


def dot_tn(a, b):
    return lax.dot_general(a, b, (((0,), (0,)), ((), ())), preferred_element_type=F32)


def params():
    return pltpu.CompilerParams(vmem_limit_bytes=VMEM)


def cost(micros):
    return pl.CostEstimate(flops=int(micros * 1.15e9), bytes_accessed=0, transcendentals=0)


def shape(dims, kind):
    return jax.ShapeDtypeStruct(tuple(dims), kind)


def pack_kernel(n_z, blocks, qkv_ref, mod_ref, up_ref, mb_ref, qb_ref, vb_ref, ob_ref, ub_ref, db_ref, out_ref):
    shard, model3 = qkv_ref.shape
    model = model3 // 3
    width = model // blocks
    devices = n_z * blocks
    ff_shard = up_ref.shape[1] // devices
    mod_shard = mod_ref.shape[1] // devices
    lanes = out_ref.shape[2]
    qkv = qkv_ref[...].astype(F32)
    mod = mod_ref[...].astype(F32)
    up = up_ref[...].astype(F32)
    tail = [r[...].astype(F32) for r in (mb_ref, ub_ref, qb_ref, vb_ref, ob_ref, db_ref)]
    tail.append(jnp.zeros((1, lanes - sum(r.shape[1] for r in tail)), F32))
    tail = [jnp.concatenate(tail, 1)]
    spare = out_ref.shape[1] - shard - 1
    if spare:
        tail.append(jnp.zeros((spare, lanes), F32))
    for e in range(blocks):
        pieces = []
        for z in range(n_z):
            d = z * blocks + e
            pieces.append(mod[:, d * mod_shard : (d + 1) * mod_shard])
            pieces.append(up[:, d * ff_shard : (d + 1) * ff_shard])
        for i in range(3):
            pieces.append(qkv[:, i * model + e * width : i * model + (e + 1) * width])
        out_ref[e] = jnp.concatenate([jnp.concatenate(pieces, 1)] + tail, 0).astype(BF)


def pack(n_z, blocks, qkv, mod, up, biases):
    shard = qkv.shape[0]
    lanes = (qkv.shape[1] + mod.shape[1] + up.shape[1]) // blocks
    rows = -(-(shard + 1) // 8) * 8
    return pl.pallas_call(
        functools.partial(pack_kernel, n_z, blocks),
        out_shape=shape((blocks, rows, lanes), BF),
        compiler_params=params(),
        cost_estimate=cost(3),
    )(qkv, mod, up, *[b.reshape(1, -1) for b in biases])


def unpack_kernel(n_z, shard, bias_lanes, got_ref, qkv_out, z_out):
    blocks = got_ref.shape[0]
    lanes = z_out.shape[2]
    got = [got_ref[e].astype(F32) for e in range(blocks)]
    whole = jnp.concatenate([g[:shard] for g in got], 0)
    qkv_out[...] = whole[:, n_z * lanes :].astype(BF)
    rows = [g[shard : shard + 1, :lanes] for g in got]
    rest = bias_lanes - lanes
    rows += [jnp.concatenate([g[shard : shard + 1, lanes:bias_lanes], jnp.zeros((1, lanes - rest), F32)], 1) for g in got]
    for z in range(n_z):
        z_out[z] = jnp.concatenate([whole[:, z * lanes : (z + 1) * lanes]] + rows, 0).astype(BF)


def unpack(got, n_z, shard, lanes, bias_lanes):
    blocks = got.shape[0]
    rows = blocks * shard
    return pl.pallas_call(
        functools.partial(unpack_kernel, n_z, shard, bias_lanes),
        out_shape=[
            shape((rows, got.shape[2] - n_z * lanes), BF), shape((n_z, rows + 2 * blocks, lanes), BF),
        ],
        compiler_params=params(),
        cost_estimate=cost(3),
    )(got)


def turn_kernel(n_z, rows, cuts, at_ref, *refs):
    got = refs[:n_z]
    outs, held = refs[n_z:-1], refs[-1]
    for k in range(n_z):
        held[at_ref[0] ^ k] = got[k][...]
    whole = jnp.concatenate([held[z, :rows].astype(F32).T for z in range(n_z)], 1)
    for i, out in enumerate(outs[: len(cuts) - 1]):
        out[...] = whole[cuts[i] : cuts[i + 1]].astype(BF)
    if len(outs) == len(cuts):
        outs[-1][...] = held[:, rows:]


def turn(z_at, got, rows, cuts):
    n_z = len(got)
    outs = [shape((cuts[i + 1] - cuts[i], rows * n_z), BF) for i in range(len(cuts) - 1)]
    if got[0].shape[0] > rows:
        outs.append(shape((n_z, got[0].shape[0] - rows, got[0].shape[1]), BF))
    return pl.pallas_call(
        functools.partial(turn_kernel, n_z, rows, cuts),
        in_specs=[pl.BlockSpec(memory_space=pltpu.SMEM)] + [pl.BlockSpec(memory_space=pltpu.VMEM)] * n_z,
        out_shape=outs,
        scratch_shapes=[pltpu.VMEM((n_z,) + got[0].shape, BF)],
        compiler_params=params(),
        cost_estimate=cost(3),
    )(z_at, *got)


def join_kernel(n_z, at_ref, *refs):
    got, (out, held) = refs[:n_z], refs[n_z:]
    for k in range(n_z):
        held[at_ref[0] ^ k] = got[k][...]
    out[...] = jnp.concatenate([held[z].astype(F32) for z in range(n_z)], 0).astype(BF)


def join(z_at, got):
    n_z = len(got)
    rows, model = got[0].shape
    return pl.pallas_call(
        functools.partial(join_kernel, n_z),
        in_specs=[pl.BlockSpec(memory_space=pltpu.SMEM)] + [pl.BlockSpec(memory_space=pltpu.VMEM)] * n_z,
        out_shape=shape((n_z * rows, model), BF),
        scratch_shapes=[pltpu.VMEM((n_z, rows, model), BF)],
        compiler_params=params(),
        cost_estimate=cost(3),
    )(z_at, *got)


def split_kernel(n_z, width, n_in, *refs):
    total = refs[0][...].astype(F32)
    for ref in refs[1:n_in]:
        total = total + ref[...].astype(F32)
    qkv_out, out_out = refs[n_in:]
    model = total.shape[1]
    part = width // n_z
    turned = total[: 3 * width].T
    rows = model // n_z
    bias = total[4 * width : 4 * width + 1]
    for z in range(n_z):
        qkv_out[z] = turned[z * rows : (z + 1) * rows].astype(BF)
        pieces = [total[3 * width + z * part : 3 * width + (z + 1) * part]]
        for i in range(4):
            at = i * width + z * part
            pieces.append(jnp.concatenate([bias[:, at : at + part], jnp.zeros((1, model - part), F32)], 1))
        spare = out_out.shape[1] - part - 4
        if spare:
            pieces.append(jnp.zeros((spare, model), F32))
        out_out[z] = jnp.concatenate(pieces, 0).astype(BF)


def split_parts(values, n_z):
    rows, model = values[0].shape
    width = (rows - 16) // 4
    out_rows = -(-(width // n_z + 4) // 8) * 8
    return pl.pallas_call(
        functools.partial(split_kernel, n_z, width, len(values)),
        out_shape=[shape((n_z, model // n_z, 3 * width), BF), shape((n_z, out_rows, model), BF)],
        compiler_params=params(),
        cost_estimate=cost(3),
    )(*values)


def deal_kernel(n_in, blocks, *refs):
    sums = []
    for i in range(2):
        total = refs[i * n_in][...].astype(F32)
        for ref in refs[i * n_in + 1 : (i + 1) * n_in]:
            total = total + ref[...].astype(F32)
        sums.append(total)
    total = jnp.concatenate(sums, 1)
    rows = total.shape[0] // blocks
    for e in range(blocks):
        refs[2 * n_in][e] = total[e * rows : (e + 1) * rows].astype(BF)


def deal(first, second, blocks):
    rows = first[0].shape[0]
    lanes = first[0].shape[1] + second[0].shape[1]
    return pl.pallas_call(
        functools.partial(deal_kernel, len(first), blocks),
        out_shape=shape((blocks, rows // blocks, lanes), BF),
        compiler_params=params(),
        cost_estimate=cost(3),
    )(*first, *second)


def turn_up_kernel(n_z, at_ref, *refs):
    got, (out, held) = refs[:n_z], refs[n_z:]
    for t in range(n_z):
        total = got[t][0].astype(F32)
        for s in range(1, got[t].shape[0]):
            total = total + got[t][s].astype(F32)
        held[lax.rem(at_ref[0] - t + n_z, n_z)] = total
    turned = jnp.concatenate([held[z].T for z in range(n_z)], 1)
    rows = out.shape[1]
    for z in range(n_z):
        out[z] = turned[z * rows : (z + 1) * rows].astype(BF)


def turn_up(z_at, got):
    n_z = len(got)
    _, ff, model = got[0].shape
    return pl.pallas_call(
        functools.partial(turn_up_kernel, n_z),
        in_specs=[pl.BlockSpec(memory_space=pltpu.SMEM)] + [pl.BlockSpec(memory_space=pltpu.VMEM)] * n_z,
        out_shape=shape((n_z, model // n_z, n_z * ff), BF),
        scratch_shapes=[pltpu.VMEM((n_z, ff, model), F32)],
        compiler_params=params(),
        cost_estimate=cost(3),
    )(z_at, *got)


def columns_kernel(groups, n_in, *refs):
    for out, (source, rows, start, size, count) in zip(refs[n_in:], groups):
        ref = refs[source]
        pieces = []
        for i in range(count):
            for n in range(ref.shape[0]):
                pieces.append(ref[n].astype(F32)[:rows, start + i * size : start + (i + 1) * size])
        out[...] = jnp.concatenate(pieces, 1)


def columns(sources, groups):
    return pl.pallas_call(
        functools.partial(columns_kernel, groups, len(sources)),
        out_shape=[shape((rows, sources[i].shape[0] * size * count), F32) for i, rows, _, size, count in groups],
        compiler_params=params(),
        cost_estimate=cost(3),
    )(*sources)


def mod_columns_kernel(early_ref, late_ref, out):
    shard = out.shape[0]
    pieces = []
    for ref in (early_ref, late_ref):
        for i in range(ref.shape[2] // shard):
            for n in range(ref.shape[0]):
                pieces.append(ref[n].astype(F32)[:shard, i * shard : (i + 1) * shard])
    out[...] = jnp.concatenate(pieces, 1)


def mod_columns(early, late, shard):
    return pl.pallas_call(
        mod_columns_kernel,
        out_shape=[shape((shard, 6 * shard * early.shape[0]), F32)],
        compiler_params=params(),
        cost_estimate=cost(3),
    )(early, late)


def place_kernel(at_ref, *refs):
    out = refs[-1]
    for k, ref in enumerate(refs[:-1]):
        out[at_ref[0] ^ k] = ref[...]


def place(at, got):
    return pl.pallas_call(
        place_kernel,
        in_specs=[pl.BlockSpec(memory_space=pltpu.SMEM)] + [pl.BlockSpec(memory_space=pltpu.VMEM)] * len(got),
        out_shape=shape((len(got),) + got[0].shape, got[0].dtype),
        compiler_params=params(),
        cost_estimate=cost(3),
    )(at, *got)


def attn_fwd_kernel(head_size, h_ref, w_a, w_b, qb_ref, vb_ref, segc_ref, segr_ref, *rest):
    q_out, k_out, v_out, att_out, lse_out = rest[-5:]
    width = qb_ref.shape[-1]
    length = segr_ref.shape[-1]
    model = h_ref.shape[-1]
    h = h_ref[...].reshape(length, model)
    allowed = segc_ref[0] == segr_ref[0]
    scale = head_size ** (-0.5)
    part = q_out.shape[1:]
    for n, w_ref in enumerate((w_a, w_b)):
        qkv = dot_nt(h, w_ref[...])
        q = (qkv[:, :width] + qb_ref[n]).astype(BF)
        k = qkv[:, width : 2 * width].astype(BF)
        v = (qkv[:, 2 * width :] + vb_ref[n]).astype(BF)
        q_out[n] = q.reshape(part)
        k_out[n] = k.reshape(part)
        v_out[n] = v.reshape(part)
        pieces = []
        for i in range(width // head_size):
            cut = slice(i * head_size, (i + 1) * head_size)
            score = jnp.where(allowed, dot_nt(k[:, cut], q[:, cut]) * scale, -1e30)
            top = jnp.max(score, 0, keepdims=True)
            prob = jnp.exp(score - top)
            total = jnp.sum(prob, 0, keepdims=True)
            out_t = dot_tn(v[:, cut], prob.astype(BF)) * (1.0 / total)
            pieces.append(out_t.T)
            lse_out[n, 0, i : i + 1, :] = top + jnp.log(total)
        att_out[n] = jnp.concatenate(pieces, -1).astype(BF).reshape(part)


def attn_fwd(hidden, w_a, w_b, query_bias, value_bias, seg_col, seg_row, head_size, wait):
    n_seq, rows, kept_count, model = hidden.shape
    width = query_bias.shape[-1]
    length = n_seq * kept_count
    heads = width // head_size
    token = pl.BlockSpec((n_seq, 1, kept_count, model), lambda r: (0, r, 0, 0))
    part = pl.BlockSpec((2, n_seq, 1, kept_count, width), lambda r: (0, 0, r, 0, 0))
    weight = pl.BlockSpec(w_a.shape, lambda r: (0, 0))
    bias = pl.BlockSpec((2, 1, width), lambda r: (0, 0, 0))
    part_shape = shape((2, n_seq, rows, kept_count, width), BF)
    return pl.pallas_call(
        functools.partial(attn_fwd_kernel, head_size),
        grid=(rows,),
        in_specs=[
            token, weight, weight, bias, bias,
            pl.BlockSpec((1, length, 1), lambda r: (r, 0, 0)),
            pl.BlockSpec((1, 1, length), lambda r: (r, 0, 0)),
        ]
        + [ANY] * len(wait),
        out_specs=[part, part, part, part, pl.BlockSpec((2, 1, heads, length), lambda r: (0, r, 0, 0))],
        out_shape=[part_shape] * 4 + [shape((2, rows, heads, length), F32)],
        compiler_params=params(),
        cost_estimate=cost(12),
    )(hidden, w_a, w_b, query_bias, value_bias, seg_col, seg_row, *wait)


def attn_bwd_kernel(head_size, first, n_wait, h_ref, gb_ref, w_a, w_b, o_a, o_b, q_ref, k_ref, v_ref, att_ref, lse_ref,
                    bias_ref, segc_ref, segr_ref, *rest):
    g_a, g_b, gh_out, sum_qkv, sum_out, sum_bias = rest[-6:]
    gh_in = None if first else rest[n_wait]
    width = q_ref.shape[-1]
    length = segr_ref.shape[-1]
    model = h_ref.shape[-1]
    row = pl.program_id(0)
    h = h_ref[...].reshape(length, model)
    gb = gb_ref[...].reshape(length, model)
    allowed = segc_ref[0] == segr_ref[0]
    scale = head_size ** (-0.5)
    total = None
    for n, (w_ref, o_ref) in enumerate(((w_a, o_a), (w_b, o_b))):
        grad_att = dot_nt(gb, o_ref[...]).astype(BF)
        q = q_ref[n].reshape(length, width)
        k = k_ref[n].reshape(length, width)
        v = v_ref[n].reshape(length, width)
        att = att_ref[n].reshape(length, width)
        gq, gk, gv = [], [], []
        for i in range(width // head_size):
            cut = slice(i * head_size, (i + 1) * head_size)
            score = dot_nt(k[:, cut], q[:, cut]) * scale - lse_ref[n, 0, i : i + 1, :]
            prob = jnp.exp(jnp.where(allowed, score, -1e30))
            grad_prob = dot_nt(v[:, cut], grad_att[:, cut])
            inner = jnp.sum(prob * grad_prob, 0, keepdims=True)
            grad_score = (prob * (grad_prob - inner)).astype(BF)
            gq.append((dot_tn(k[:, cut], grad_score) * scale).T)
            gk.append(dot_nn(grad_score, q[:, cut]) * scale)
            gv.append(dot_nn(prob.astype(BF), grad_att[:, cut]))
        grad_qkv = jnp.concatenate(gq + gk + gv, -1).astype(BF)
        term = dot_nn(grad_qkv, w_ref[...])
        total = term if total is None else total + term
        term_qkv = dot_tn(grad_qkv, h)
        term_out = dot_tn(att, gb)
        term_bias = jnp.sum(grad_qkv.astype(F32), 0, keepdims=True)

        @pl.when(row == 0)
        def _():
            sum_qkv[n] = term_qkv
            sum_out[n] = term_out
            sum_bias[n] = term_bias

        @pl.when(row != 0)
        def _():
            sum_qkv[n] += term_qkv
            sum_out[n] += term_out
            sum_bias[n] += term_bias

    if first:
        gh_out[...] = total.reshape(gh_out.shape)
    else:
        gh_out[...] = gh_in[...] + total.reshape(gh_out.shape)

    @pl.when(row == pl.num_programs(0) - 1)
    def _():
        for n, g_ref in enumerate((g_a, g_b)):
            g_ref[: 3 * width] = sum_qkv[n].astype(BF)
            g_ref[3 * width : 4 * width] = sum_out[n].astype(BF)
            biases = jnp.concatenate(
                [sum_bias[n, :, :width], sum_bias[n, :, 2 * width :], bias_ref[n],
                 jnp.zeros((1, model - 4 * width), F32)], -1
            )
            g_ref[4 * width :] = jnp.broadcast_to(biases, (16, model)).astype(BF)


def attn_bwd(hidden, grad_branch, w_a, w_b, o_a, o_b, saved, bias, seg_col, seg_row, head_size, grad_hidden, wait):
    q, k, v, att, lse = saved
    n_seq, rows, kept_count, model = hidden.shape
    width = q.shape[-1]
    length = n_seq * kept_count
    heads = width // head_size
    first = grad_hidden is None
    token = pl.BlockSpec((n_seq, 1, kept_count, model), lambda r: (0, r, 0, 0))
    part = pl.BlockSpec((2, n_seq, 1, kept_count, width), lambda r: (0, 0, r, 0, 0))
    weight = pl.BlockSpec(w_a.shape, lambda r: (0, 0))
    out_weight = pl.BlockSpec(o_a.shape, lambda r: (0, 0))
    out = pl.BlockSpec((4 * width + 16, model), lambda r: (0, 0))
    own = [] if first else [grad_hidden]
    return pl.pallas_call(
        functools.partial(attn_bwd_kernel, head_size, first, len(wait)),
        grid=(rows,),
        in_specs=[
            token, token, weight, weight, out_weight, out_weight, part, part, part, part,
            pl.BlockSpec((2, 1, heads, length), lambda r: (0, r, 0, 0)),
            pl.BlockSpec((2, 1, 2 * width), lambda r: (0, 0, 0)),
            pl.BlockSpec((1, length, 1), lambda r: (r, 0, 0)),
            pl.BlockSpec((1, 1, length), lambda r: (r, 0, 0)),
        ]
        + [ANY] * len(wait)
        + [token] * len(own),
        out_specs=[out, out, token],
        out_shape=[shape((4 * width + 16, model), BF)] * 2 + [shape(hidden.shape, F32)],
        scratch_shapes=[
            pltpu.VMEM((2, 3 * width, model), F32),
            pltpu.VMEM((2, width, model), F32),
            pltpu.VMEM((2, 1, 3 * width), F32),
        ],
        input_output_aliases={} if first else {14 + len(wait): 2},
        compiler_params=params(),
        cost_estimate=cost(24),
    )(hidden, grad_branch, w_a, w_b, o_a, o_b, q, k, v, att, lse, bias, seg_col, seg_row, *wait, *own)


def pick_slot(table_ref, seg, index):
    value = table_ref[0, 0, index : index + 1, :]
    for slot in range(1, table_ref.shape[1]):
        value = jnp.where(seg == slot, table_ref[0, slot, index : index + 1, :], value)
    return value


def add_slots(out_ref, index, seg, value, start):
    for slot in range(out_ref.shape[1]):
        part = jnp.sum(jnp.where(seg == slot, value, 0.0), 0, keepdims=True)
        at = (0, slot, slice(index, index + 1))
        out_ref[at] = jnp.where(start, 0.0, out_ref[at]) + part


def after_attn_kernel(n_blocks, width, x_ref, seg_ref, table_ref, ob_ref, *rest):
    att_refs = rest[: n_blocks // 2]
    w_refs = rest[n_blocks // 2 : n_blocks // 2 + n_blocks]
    br_out, mid_out, h2_out = rest[-3:]
    kept_count, model = x_ref.shape[2:]
    seg = seg_ref[0, 0]
    branch = ob_ref[...]
    for j in range(n_blocks // 2):
        for n in range(2):
            w = w_refs[j + n * (n_blocks // 2)][...]
            branch = branch + dot_nn(att_refs[j][n].reshape(kept_count, width), w)
    mid = x_ref[0, 0].astype(F32) + pick_slot(table_ref, seg, 2) * branch
    normed, _ = normalize(mid)
    br_out[0, 0] = branch
    mid_out[0, 0] = mid
    h2_out[0, 0] = (normed * (1.0 + pick_slot(table_ref, seg, 4)) + pick_slot(table_ref, seg, 3)).astype(BF)


def after_attn(inputs, seg, table, out_bias, atts, weights, wait):
    n_seq, rows, kept_count, model = inputs.shape
    width = atts[0].shape[-1]
    slots = table.shape[1]
    token = pl.BlockSpec((1, 1, kept_count, model), lambda r, j: (j, r, 0, 0))
    part = pl.BlockSpec((2, 1, 1, kept_count, width), lambda r, j: (0, j, r, 0, 0))
    weight = pl.BlockSpec((width, model), lambda r, j: (0, 0))
    return pl.pallas_call(
        functools.partial(after_attn_kernel, len(weights), width),
        grid=(rows, n_seq),
        in_specs=[
            token,
            pl.BlockSpec((1, 1, kept_count, 1), lambda r, j: (j, r, 0, 0)),
            pl.BlockSpec((1, slots, 6, model), lambda r, j: (r, 0, 0, 0)),
            pl.BlockSpec((1, model), lambda r, j: (0, 0)),
        ]
        + [part] * len(atts)
        + [weight] * len(weights)
        + [ANY] * len(wait),
        out_specs=[token] * 3,
        out_shape=[shape(inputs.shape, F32), shape(inputs.shape, F32), shape(inputs.shape, BF)],
        compiler_params=params(),
        cost_estimate=cost(15),
    )(inputs, seg, table, out_bias, *atts, *weights, *wait)


def after_mlp_kernel(mid_ref, mlp_ref, gh_ref, br_ref, ct_ref, seg_ref, table_ref, db_ref, *rest):
    res_out, gm_out, gb_out, sums_out, obias_out = rest[-5:]
    seg = seg_ref[0, 0]
    step = pl.program_id(1)
    mid = mid_ref[0, 0]
    branch_mlp = mlp_ref[0, 0] + db_ref[...]
    grad_hidden = gh_ref[0, 0]
    grad_result = ct_ref[0, 0].astype(F32)
    res_out[0, 0] = (mid + pick_slot(table_ref, seg, 5) * branch_mlp).astype(BF)
    normed, inv = normalize(mid)
    grad_mid = grad_result + norm_back(grad_hidden * (1.0 + pick_slot(table_ref, seg, 4)), normed, inv)
    gm_out[0, 0] = grad_mid
    grad_branch = (grad_mid * pick_slot(table_ref, seg, 2)).astype(BF)
    gb_out[0, 0] = grad_branch
    add_slots(sums_out, 0, seg, grad_mid * br_ref[0, 0], step == 0)
    add_slots(sums_out, 1, seg, grad_hidden, step == 0)
    add_slots(sums_out, 2, seg, grad_hidden * normed, step == 0)
    add_slots(sums_out, 3, seg, grad_result * branch_mlp, step == 0)
    start = jnp.logical_and(step == 0, pl.program_id(0) == 0)
    part = jnp.sum(grad_branch.astype(F32), 0, keepdims=True)
    obias_out[...] = jnp.where(start, 0.0, obias_out[...]) + part


def after_mlp(mid, mlp, grad_hidden, branch, cotangent, seg, table, down_bias, wait):
    n_seq, rows, kept_count, model = mid.shape
    slots = table.shape[1]
    token = pl.BlockSpec((1, 1, kept_count, model), lambda r, j: (j, r, 0, 0))
    vector = pl.BlockSpec((1, model), lambda r, j: (0, 0))
    return pl.pallas_call(
        after_mlp_kernel,
        grid=(rows, n_seq),
        in_specs=[
            token, token, token, token, token,
            pl.BlockSpec((1, 1, kept_count, 1), lambda r, j: (j, r, 0, 0)),
            pl.BlockSpec((1, slots, 6, model), lambda r, j: (r, 0, 0, 0)),
            vector,
        ]
        + [ANY] * len(wait),
        out_specs=[
            token, token, token,
            pl.BlockSpec((1, slots, 4, model), lambda r, j: (r, 0, 0, 0)),
            vector,
        ],
        out_shape=[
            shape(mid.shape, BF), shape(mid.shape, F32), shape(mid.shape, BF),
            shape((rows, slots, 4, model), F32), shape((1, model), F32),
        ],
        compiler_params=params(),
        cost_estimate=cost(21),
    )(mid, mlp, grad_hidden, branch, cotangent, seg, table, down_bias, *wait)


def last_kernel(x_ref, gh_ref, gm_ref, seg_ref, table_ref, *rest):
    gx_out, sums_out = rest[-2:]
    seg = seg_ref[0, 0]
    step = pl.program_id(1)
    grad_hidden = gh_ref[0, 0]
    normed, inv = normalize(x_ref[0, 0].astype(F32))
    back = norm_back(grad_hidden * (1.0 + pick_slot(table_ref, seg, 1)), normed, inv)
    gx_out[0, 0] = (gm_ref[0, 0] + back).astype(BF)
    add_slots(sums_out, 0, seg, grad_hidden, step == 0)
    add_slots(sums_out, 1, seg, grad_hidden * normed, step == 0)


def last_step(inputs, grad_hidden, grad_mid, seg, table, wait):
    n_seq, rows, kept_count, model = inputs.shape
    slots = table.shape[1]
    token = pl.BlockSpec((1, 1, kept_count, model), lambda r, j: (j, r, 0, 0))
    return pl.pallas_call(
        last_kernel,
        grid=(rows, n_seq),
        in_specs=[
            token, token, token,
            pl.BlockSpec((1, 1, kept_count, 1), lambda r, j: (j, r, 0, 0)),
            pl.BlockSpec((1, slots, 6, model), lambda r, j: (r, 0, 0, 0)),
        ]
        + [ANY] * len(wait),
        out_specs=[token, pl.BlockSpec((1, slots, 2, model), lambda r, j: (r, 0, 0, 0))],
        out_shape=[shape(inputs.shape, BF), shape((rows, slots, 2, model), F32)],
        compiler_params=params(),
        cost_estimate=cost(12),
    )(inputs, grad_hidden, grad_mid, seg, table, *wait)


def mlp_kernel(n_up, n_down, first, n_wait, h_ref, gm_ref, ub_ref, *rest):
    up_refs = rest[:n_up]
    down_refs = rest[n_up : n_up + n_down]
    if first:
        mlp_in = gh_in = None
    else:
        mlp_in, gh_in = rest[n_up + n_down + n_wait : n_up + n_down + n_wait + 2]
    mlp_out, gh_out, own_out, other_out, gub_out, up, down, sum_up, sum_down, sum_bias = rest[-10:]
    step = pl.program_id(0)
    model = h_ref.shape[-1]

    @pl.when(step == 0)
    def _():
        for refs, whole in ((up_refs, up), (down_refs, down)):
            at = 0
            for ref in refs:
                block = ref[...].reshape(-1, model)
                whole[at : at + block.shape[0]] = block
                at += block.shape[0]

    h = h_ref[...]
    gm = gm_ref[...]
    pre = dot_nt(h, up[...]) + ub_ref[0]
    square = pre * pre
    tanh_part = jnp.tanh(GELU_C * pre * (1.0 + GELU_A * square))
    half = 0.5 * (1.0 + tanh_part)
    activated = (pre * half).astype(BF)
    slope = half + 0.5 * pre * (1.0 - tanh_part * tanh_part) * GELU_C * (1.0 + 3.0 * GELU_A * square)
    grad_pre = (dot_nt(gm, down[...]) * slope).astype(BF)
    mlp_term = dot_nn(activated, down[...])
    gh_term = dot_nn(grad_pre, up[...])
    mlp_out[...] = mlp_term if first else mlp_in[...] + mlp_term
    gh_out[...] = gh_term if first else gh_in[...] + gh_term
    up_term = dot_tn(grad_pre, h)
    down_term = dot_tn(activated, gm)
    bias_term = jnp.sum(grad_pre.astype(F32), 0, keepdims=True)

    @pl.when(step == 0)
    def _():
        sum_up[...] = up_term
        sum_down[...] = down_term
        sum_bias[...] = bias_term

    @pl.when(step != 0)
    def _():
        sum_up[...] += up_term
        sum_down[...] += down_term
        sum_bias[...] += bias_term

    @pl.when(step == pl.num_programs(0) - 1)
    def _():
        half_rows = sum_up.shape[0] // 2
        own_out[0] = sum_up[:half_rows].astype(BF)
        own_out[1] = sum_down[:half_rows].astype(BF)
        other_out[0] = sum_up[half_rows:].astype(BF)
        other_out[1] = sum_down[half_rows:].astype(BF)
        gub_out[...] = sum_bias[...]


def mlp_step(hidden, grad_mlp, up_bias, ups, downs, sums, wait):
    count, model = hidden.shape
    chunk = min(512, count)
    width = sum(u.shape[0] * u.shape[1] for u in ups)
    first = sums is None
    own = [] if first else list(sums)
    token = pl.BlockSpec((chunk, model), lambda i: (i, 0))
    weights = [pl.BlockSpec(u.shape, lambda i: (0, 0, 0)) for u in ups + downs]
    grads = pl.BlockSpec((2, width // 2, model), lambda i: (0, 0, 0))
    inputs = 3 + len(ups) + len(downs) + len(wait)
    return pl.pallas_call(
        functools.partial(mlp_kernel, len(ups), len(downs), first, len(wait)),
        grid=(count // chunk,),
        in_specs=[token, token, pl.BlockSpec((1, 1, width), lambda i: (0, 0, 0))]
        + weights
        + [ANY] * len(wait)
        + [token] * len(own),
        out_specs=[token, token, grads, grads, pl.BlockSpec((1, width), lambda i: (0, 0))],
        out_shape=[
            shape((count, model), F32), shape((count, model), F32),
            shape((2, width // 2, model), BF), shape((2, width // 2, model), BF), shape((1, width), F32),
        ],
        scratch_shapes=[
            pltpu.VMEM((width, model), BF), pltpu.VMEM((width, model), BF),
            pltpu.VMEM((width, model), F32), pltpu.VMEM((width, model), F32), pltpu.VMEM((1, width), F32),
        ],
        input_output_aliases={} if first else {inputs: 0, inputs + 1: 1},
        compiler_params=params(),
        cost_estimate=cost(32),
    )(hidden, grad_mlp, up_bias, *ups, *downs, *wait, *own)


def tie(value, *after):
    return lax.optimization_barrier((value,) + after)[0]


def body(
    n_z, n_seq,
    tokens, conditioning, segments, kept, cotangent,
    mod_weight, mod_bias, qkv_weight, query_bias, value_bias, out_weight, out_bias,
    up_weight, up_bias, down_weight, down_bias,
):
    row_count, seq_tokens, model = tokens.shape
    kept_count = kept.shape[1]
    slots = conditioning.shape[1]
    head_size = model // HEADS
    rows = row_count // n_seq
    shard = qkv_weight.shape[0]
    blocks = 2 * n_seq
    devices = n_z * blocks
    width = model // blocks
    part = width // n_z
    flat = n_seq * rows * kept_count
    ff_shard = down_weight.shape[0]
    z_at = lax.axis_index("z")
    core_at = lax.axis_index("core")
    seq_at = lax.axis_index("seq")
    block_at = core_at * n_seq + seq_at
    relative = block_at ^ jnp.arange(blocks)
    z_relative = z_at ^ jnp.arange(n_z)
    seq_relative = seq_at ^ jnp.arange(n_seq)
    core_relative = core_at ^ jnp.arange(2)
    z_ring = (z_at - jnp.arange(n_z)) % n_z
    seq_scalar = seq_at.reshape(1).astype(jnp.int32)
    z_scalar = z_at.reshape(1).astype(jnp.int32)
    mod_shard = 6 * shard

    def over_core(value):
        return lax.ppermute(value, "core", [(0, 1), (1, 0)])

    def over_seq(value, by):
        return lax.ppermute(value, "seq", [(i, i ^ by) for i in range(n_seq)])

    def over_z(value, by):
        return lax.ppermute(value, "z", [(i, i ^ by) for i in range(n_z)])

    def shift_z(value, by):
        return lax.ppermute(value, "z", [(i, (i + by) % n_z) for i in range(n_z)])

    def all_to_all(value):
        return lax.all_to_all(value, EVERY, 0, 0, tiled=True)

    def dense_to_all(value):
        return lax.all_to_all(value, DENSE, 0, 0, tiled=True)

    def to_z(value):
        mine = [lax.dynamic_index_in_dim(value, z_at ^ k, 0, keepdims=False) for k in range(n_z)]
        return [mine[0]] + [over_z(mine[k], k) for k in range(1, n_z)]

    def sum_of(values):
        total = values[0].astype(F32)
        for value in values[1:]:
            total = total + value.astype(F32)
        return total

    def plane(value):
        return [value] + [over_seq(value, j) for j in range(1, n_seq)]

    def seq_to_all(value):
        return lax.all_to_all(value, "seq", 0, 0, tiled=True)

    def gather_seq(value):
        return seq_to_all(jnp.broadcast_to(value[None], (n_seq,) + value.shape))

    def to_rows(value):
        return seq_to_all(value.reshape((n_seq, rows) + value.shape[1:]))

    def from_rows(value):
        return seq_to_all(value).reshape((row_count,) + value.shape[2:])

    first_cols = pack(
        n_z, blocks, qkv_weight, mod_weight, up_weight, (mod_bias, query_bias, value_bias, out_bias, up_bias, down_bias)
    )
    first_got = dense_to_all(first_cols)
    down_got = plane(tie(down_weight, first_cols))

    places = jnp.arange(seq_tokens, dtype=jnp.int32)
    kept = tie(kept, first_cols)
    hits = kept[:, :, None] == places
    pick = hits.astype(BF)
    kept_here = jnp.any(hits, 1)

    def pick_kept(value):
        return jnp.einsum("rkt,rtd->rkd", pick, value, preferred_element_type=F32).astype(BF)

    def put_kept(value, base):
        spread = jnp.einsum("rkt,rkd->rtd", pick, value, preferred_element_type=F32).astype(BF)
        return jnp.where(kept_here[:, :, None], spread, base)

    picked = pick_kept(tokens)
    picked_ct = pick_kept(cotangent)
    inputs = to_rows(tie(picked, first_got))

    cond_float = conditioning.astype(F32).reshape(row_count * slots, model)
    cond_act = (cond_float / (1.0 + jnp.exp(-cond_float))).astype(BF)
    act_other = over_core(cond_act)
    act_pair = jnp.concatenate([jnp.where(core_at == 0, cond_act, act_other), jnp.where(core_at == 0, act_other, cond_act)])
    act_got = [act_pair] + [over_z(act_pair, k) for k in range(1, n_z)]
    act_all = jnp.take(jnp.stack(act_got), z_relative, axis=0).reshape(-1, model)

    numbers = jnp.arange(slots, dtype=jnp.int32)
    query_seg = jnp.sum(jnp.where(hits, segments[:, None, :], 0), -1)
    kept_hits = jnp.sum((query_seg[:, :, None] == numbers).astype(jnp.int32), 1)
    all_hits = jnp.sum((segments[:, :, None] == numbers).astype(jnp.int32), 1)
    small = jnp.concatenate([query_seg, kept_hits, all_hits - kept_hits], -1)
    small_got = plane(small)
    small = jnp.take(jnp.stack(small_got), seq_relative, axis=0)
    sample_counts = jnp.sum(small[:, :, kept_count:], 0).reshape(row_count, 2, slots).transpose(0, 2, 1)
    seg = lax.dynamic_slice_in_dim(small[:, :, :kept_count], seq_at * rows, rows, 1)
    seg_rows = seg.transpose(1, 0, 2).reshape(rows, 1, n_seq * kept_count)
    seg_cols = seg_rows.reshape(rows, n_seq * kept_count, 1)
    seg_tokens = seg.reshape(n_seq, rows, kept_count, 1)

    qkv_rows, z_cols = unpack(tie(first_got, *act_got[1:], *small_got[1:], *down_got[1:], picked), n_z, shard, mod_shard + ff_shard, mod_shard + ff_shard + 4 * shard)
    qkv_got = [qkv_rows] + [over_z(qkv_rows, k) for k in range(1, n_z)]
    (w_own,) = turn(z_scalar, qkv_got, blocks * shard, (0, 3 * width))
    z_got = to_z(tie(z_cols, *qkv_got[1:]))
    mod_cols, up_part, bias_got = turn(z_scalar, z_got, blocks * shard, (0, mod_shard, mod_shard + ff_shard))
    bias_got = bias_got.astype(F32)
    mod_b = bias_got[:, :blocks, :mod_shard].reshape(-1)
    up_b = bias_got[:, :blocks, mod_shard:].reshape(-1)
    query_b, value_b, out_b, down_b = [
        bias_got[:, blocks:, i * shard : (i + 1) * shard].reshape(-1) for i in range(4)
    ]

    mod_part = tie(dot_nt(act_all, mod_cols), inputs).reshape(devices, rows * slots, mod_shard)
    modulation = tie(all_to_all(mod_part), picked_ct).transpose(1, 0, 2).reshape(rows * slots, 6 * model) + mod_b
    table = modulation.reshape(rows, slots, 6, model)

    def token_mod(index):
        value = table[None, :, None, 0, index]
        for slot in range(1, slots):
            value = jnp.where(seg_tokens == slot, table[None, :, None, slot, index], value)
        return value

    hidden_one = (normalize(inputs.astype(F32))[0] * (1.0 + token_mod(1)) + token_mod(0)).astype(BF)

    spread_out = []
    for d in range(devices):
        z, c, s = d % n_z, (d // n_z) // n_seq, (d // n_z) % n_seq
        spread_out.append((d, (z * 2 + c) * n_seq + s))
    out_part = lax.ppermute(out_weight, EVERY, spread_out)
    out_part = tie(out_part, *z_got[1:])
    out_got = [out_part] + [over_z(out_part, k) for k in range(1, n_z)]
    o_own = join(z_scalar, out_got)
    w_all = plane(w_own)
    w_all = w_all + [over_core(w) for w in w_all]

    down_ring = [place(seq_scalar, down_got)]
    up_ring = [gather_seq(tie(up_part, hidden_one))]
    down_ring.append(shift_z(tie(down_ring[0], *out_got[1:]), 1))
    for t in range(2, n_z):
        if t == 2:
            down_ring.append(shift_z(tie(down_ring[1], hidden_one), 1))
            up_ring.append(shift_z(tie(up_ring[0], down_ring[2]), 1))
        else:
            down_ring.append(shift_z(tie(down_ring[-1], up_ring[-1]), 1))
        up_ring.append(shift_z(tie(up_ring[-1], down_ring[-1]) if t > 2 else up_ring[-1], 1))
    while len(up_ring) < n_z:
        up_ring.append(shift_z(up_ring[-1], 1))
    down_other = [over_core(value) for value in down_ring]
    up_other = [over_core(value) for value in up_ring]
    o_all = plane(tie(o_own, hidden_one))
    o_all = o_all + [over_core(o) for o in o_all]

    def by_block(value):
        return jnp.take(value.reshape(blocks, 1, width), relative, axis=0)

    query_b, value_b = by_block(query_b), by_block(value_b)
    up_b = jnp.take(up_b.reshape(n_z, 2, n_seq * ff_shard), core_relative, axis=1)
    up_b = jnp.take(up_b, z_ring, axis=0).reshape(n_z, 1, blocks * ff_shard)

    def pair(value, j):
        return jnp.stack([value[j], value[j + n_seq]])

    saved = []
    for j in range(n_seq):
        saved.append(attn_fwd(
            hidden_one, w_all[j], w_all[j + n_seq], pair(query_b, j), pair(value_b, j), seg_cols, seg_rows, head_size, [],
        ))
    branch_attn, mid, hidden_two = after_attn(
        inputs, seg_tokens, table, out_b.reshape(1, -1), [s[3] for s in saved], o_all, [],
    )
    grad_result = to_rows(tie(picked_ct, up_ring[0]))
    grad_mlp = (grad_result.astype(F32) * token_mod(5)).astype(BF)
    grad_down_bias = jnp.sum(grad_mlp.astype(F32), (0, 1, 2))

    order = list(range(n_z))
    hidden_flat = hidden_two.reshape(flat, model)
    grad_flat = grad_mlp.reshape(flat, model)
    sums = None
    cores, sends, planes, down_sums, grad_up_bias = [], [], [], {}, {}
    ring = []
    for at, t in enumerate(order):
        ups = [up_ring[t], up_other[t]]
        downs = [down_ring[t], down_other[t]]
        if ff_shard % 16:
            ups = [jnp.concatenate([u.reshape(-1, model) for u in ups])[None]]
            downs = [jnp.concatenate([d.reshape(-1, model) for d in downs])[None]]
        wait = []
        if at >= 2:
            wait.extend(sends[at - 2])
        if at >= 3:
            wait.append(planes[at - 3])
        mlp_sum, gh_sum, own, other, grad_up_bias[t] = mlp_step(
            hidden_flat, grad_flat, up_b[t : t + 1], ups, downs, sums, wait
        )
        sums = (mlp_sum, gh_sum)
        cores.append(over_core(other))
        both = (own.astype(F32) + cores[at].astype(F32)).reshape(2, n_seq, ff_shard, model)
        sends.append([both[0].astype(BF)])
        planes.append(seq_to_all(sends[at][0]))
        down_sums[t] = both[1]
        if t and len(ring) == t - 1:
            value = both[1] if t == 1 else both[1] + ring[-1].astype(F32)
            sends[at].append(value.astype(BF))
            ring.append(shift_z(sends[at][1], 1))

    last = n_z - 1
    res, grad_mid, grad_branch, sums_late, grad_out_bias = after_mlp(
        mid, sums[0].reshape(mid.shape), sums[1].reshape(mid.shape), branch_attn, grad_result, seg_tokens, table,
        down_b.reshape(1, -1), sends[last - 1] + [planes[last - 2]],
    )

    def natural_block(value):
        return by_block(value.reshape(-1))

    late_bias = jnp.concatenate([natural_block(grad_out_bias), natural_block(grad_down_bias)], -1)
    late = sums_late.reshape(rows * slots, 4, devices, shard).transpose(2, 0, 1, 3).reshape(devices, rows * slots, -1)
    late = late.astype(BF)
    waits = sends[last] + [planes[last - 1]]
    grad_hidden = None
    w_cores, w_values, w_planes = [], [], []
    for at, j in enumerate([n_seq - 1] + list(range(1, n_seq - 1)) + [0]):
        g_own, g_other, grad_hidden = attn_bwd(
            hidden_one, grad_branch, w_all[j], w_all[j + n_seq], o_all[j], o_all[j + n_seq], saved[j],
            pair(late_bias, j), seg_cols, seg_rows, head_size, grad_hidden, waits,
        )
        waits = []
        if at == 0:
            waits = [planes[last]]
            late = all_to_all(tie(late, g_own)).reshape(-1, 4 * shard)
            res = tie(res, g_own)
            res_mine = [lax.dynamic_index_in_dim(res, seq_at ^ k, 0, keepdims=False) for k in range(n_seq)]
            res_got = [res_mine[0]] + [over_seq(res_mine[k], k) for k in range(1, n_seq)]
            down_last = (down_sums[0] + ring[-1].astype(F32)).astype(BF)
        elif at == 1:
            late_mod = dot_tn(act_all, tie(late, g_own)).astype(BF).reshape(devices, shard, 4 * shard)
            natural = jnp.stack([grad_up_bias[t] for t in range(n_z)]).reshape(n_z, 2, n_seq * ff_shard)
            natural = jnp.take(jnp.take(natural, core_relative, axis=1), z_ring, axis=0).reshape(devices, 1, ff_shard)
            late_got = all_to_all(jnp.concatenate([late_mod, natural.astype(BF)], 1))
            up_bias_grad = jnp.sum(late_got[:, shard].astype(F32), 0)
            up_turned = turn_up(z_scalar, [planes[order.index(t)] for t in range(n_z)])
            up_parts = to_z(up_turned)
            waits = [ring[-1], late, up_turned] + res_got[1:]
        elif at == 2:
            waits = [late_got]
            down_parts = seq_to_all(tie(down_last, g_own))
            down_grad = jnp.sum(down_parts.astype(F32), 0)
        elif at == 3:
            waits = [down_parts] + up_parts[1:]
        w_cores.append(over_core(g_other))
        w_values.append((g_own.astype(F32) + w_cores[at].astype(F32)).astype(BF))
        w_planes.append(over_seq(w_values[at], j) if j else w_values[at])
        if at >= 1:
            waits.append(w_values[at - 1])
        if at == n_seq - 2:
            waits.append(w_values[at])

    grad_x, sums_early = last_step(inputs, grad_hidden, grad_mid, seg_tokens, table, waits)
    grad_mine = [lax.dynamic_index_in_dim(grad_x, seq_at ^ k, 0, keepdims=False) for k in range(n_seq)]
    grad_got = [grad_mine[0]] + [over_seq(grad_mine[k], k) for k in range(1, n_seq)]

    def in_place(got):
        return place(seq_scalar, got).reshape((row_count,) + got[0].shape[1:])

    res_got[0] = tie(res_got[0], grad_x)
    output = put_kept(in_place(res_got), tokens)
    tokens_grad = put_kept(in_place(grad_got), cotangent)

    qkv_parts, out_parts = split_parts(w_planes, n_z)
    qkv_parts = to_z(qkv_parts)
    out_parts = to_z(out_parts)
    back_out = lax.ppermute(sum_of(out_parts).astype(BF), EVERY, [(t, d) for d, t in spread_out]).astype(F32)
    out_grad = back_out[:part]
    small_grads = back_out[part : part + 4, :part]

    early = sums_early.reshape(rows * slots, 2, devices, shard).transpose(2, 0, 1, 3).reshape(devices, rows * slots, -1)
    early = all_to_all(early.astype(BF)).reshape(-1, 2 * shard)
    early_mod = dot_tn(act_all, early).astype(BF).reshape(devices, shard, 2 * shard)
    mod_sums = jnp.concatenate([jnp.sum(sums_early, (0, 1)), jnp.sum(sums_late, (0, 1))]).reshape(devices, 6 * shard)
    mod_sums = mod_sums.astype(BF).reshape(devices, 3, 2 * shard)
    mod_got = all_to_all(jnp.concatenate([early_mod, mod_sums], 1))
    mod_bias_grad = jnp.sum(mod_got[:, shard:].reshape(devices, -1).astype(F32), 0)
    dense_got = dense_to_all(deal(qkv_parts, up_parts, blocks))
    qkv_grad, up_grad = columns(
        [dense_got], [(0, shard, 0, width, 3), (0, shard, 3 * width, ff_shard, n_z)]
    )
    (mod_grad,) = mod_columns(mod_got, late_got, shard)
    return (
        output, tokens_grad, mod_grad, mod_bias_grad, qkv_grad, small_grads[0], small_grads[1],
        out_grad, small_grads[2], up_grad, up_bias_grad, down_grad, small_grads[3], sample_counts,
    )


def solution(mesh):
    n_batch, n_seq = mesh.shape["batch"], mesh.shape["seq"]
    split = Mesh(mesh.devices.reshape(n_batch // 2, 2, n_seq), ("z", "core", "seq"))
    batch = ("z", "core")
    both = ("z", "core", "seq")
    row_split = P(batch, "seq", None)
    matrix = P(both, None)
    vector = P(both)
    return jax.shard_map(
        functools.partial(body, n_batch // 2, n_seq),
        mesh=split,
        in_specs=(
            row_split, P(batch, None, None), P(batch, "seq"), P(batch, "seq"), row_split,
            matrix, vector, matrix, vector, vector, matrix, vector, matrix, vector, matrix, vector,
        ),
        out_specs=(
            row_split, row_split, matrix, vector, matrix, vector, vector,
            matrix, vector, matrix, vector, matrix, vector, P(batch, None, None),
        ),
        check_vma=False,
    )
```

```python
import functools

import jax
import jax.numpy as jnp
from jax import lax
from jax.experimental import pallas as pl
from jax.experimental.pallas import tpu as pltpu
from jax.sharding import Mesh
from jax.sharding import PartitionSpec as P

HEADS = 16
EPS = 1e-06
GELU_C = 0.7978845608028654
GELU_A = 0.044715
BF = jnp.bfloat16
F32 = jnp.float32
VMEM = 58 * 1024 * 1024
ANY = pl.BlockSpec(memory_space=pl.ANY)
SMEM = pl.BlockSpec(memory_space=pltpu.SMEM)
EVERY = ("z", "core", "seq")
DENSE = ("core", "seq")


def normalize(values):
    center = values - jnp.mean(values, -1, keepdims=True)
    scale_inv = lax.rsqrt(jnp.mean(center * center, -1, keepdims=True) + EPS)
    return (center * scale_inv, scale_inv)


def norm_back(grad_norm, normed, scale_inv):
    return scale_inv * (
        grad_norm
        - jnp.mean(grad_norm, -1, keepdims=True)
        - normed * jnp.mean(grad_norm * normed, -1, keepdims=True)
    )


def dot_nn(a, b):
    return lax.dot_general(a, b, (((1,), (0,)), ((), ())), preferred_element_type=F32)


def dot_nt(a, b):
    return lax.dot_general(a, b, (((1,), (1,)), ((), ())), preferred_element_type=F32)


def dot_tn(a, b):
    return lax.dot_general(a, b, (((0,), (0,)), ((), ())), preferred_element_type=F32)


def params():
    return pltpu.CompilerParams(vmem_limit_bytes=VMEM)


def cost(micros):
    return pl.CostEstimate(flops=int(micros * 1.15e9), bytes_accessed=0, transcendentals=0)


def shape(dims, kind):
    return jax.ShapeDtypeStruct(tuple(dims), kind)


def pack_kernel(n_z, blocks, qkv_ref, mod_ref, up_ref, mb_ref, qb_ref, vb_ref, ob_ref, ub_ref, db_ref, out_ref):
    shard, model3 = qkv_ref.shape
    model = model3 // 3
    width = model // blocks
    devices = n_z * blocks
    ff_shard = up_ref.shape[1] // devices
    mod_shard = mod_ref.shape[1] // devices
    lanes = out_ref.shape[2]
    qkv = qkv_ref[...].astype(F32)
    mod = mod_ref[...].astype(F32)
    up = up_ref[...].astype(F32)
    tail = [r[...].astype(F32) for r in (mb_ref, ub_ref, qb_ref, vb_ref, ob_ref, db_ref)]
    tail.append(jnp.zeros((1, lanes - sum(r.shape[1] for r in tail)), F32))
    tail = [jnp.concatenate(tail, 1)]
    spare = out_ref.shape[1] - shard - 1
    if spare:
        tail.append(jnp.zeros((spare, lanes), F32))
    for e in range(blocks):
        pieces = []
        for z in range(n_z):
            d = z * blocks + e
            pieces.append(mod[:, d * mod_shard : (d + 1) * mod_shard])
            pieces.append(up[:, d * ff_shard : (d + 1) * ff_shard])
        for i in range(3):
            pieces.append(qkv[:, i * model + e * width : i * model + (e + 1) * width])
        out_ref[e] = jnp.concatenate([jnp.concatenate(pieces, 1)] + tail, 0).astype(BF)


def pack(n_z, blocks, qkv, mod, up, biases):
    shard = qkv.shape[0]
    lanes = (qkv.shape[1] + mod.shape[1] + up.shape[1]) // blocks
    rows = -(-(shard + 1) // 8) * 8
    return pl.pallas_call(
        functools.partial(pack_kernel, n_z, blocks),
        out_shape=shape((blocks, rows, lanes), BF),
        compiler_params=params(),
        cost_estimate=cost(3),
    )(qkv, mod, up, *[b.reshape(1, -1) for b in biases])


def unpack_kernel(n_z, shard, bias_lanes, got_ref, qkv_out, z_out):
    blocks = got_ref.shape[0]
    lanes = z_out.shape[2]
    got = [got_ref[e].astype(F32) for e in range(blocks)]
    whole = jnp.concatenate([g[:shard] for g in got], 0)
    qkv_out[...] = whole[:, n_z * lanes :].astype(BF)
    rows = [g[shard : shard + 1, :lanes] for g in got]
    rest = bias_lanes - lanes
    rows += [jnp.concatenate([g[shard : shard + 1, lanes:bias_lanes], jnp.zeros((1, lanes - rest), F32)], 1) for g in got]
    for z in range(n_z):
        z_out[z] = jnp.concatenate([whole[:, z * lanes : (z + 1) * lanes]] + rows, 0).astype(BF)


def unpack(got, n_z, shard, lanes, bias_lanes):
    blocks = got.shape[0]
    rows = blocks * shard
    return pl.pallas_call(
        functools.partial(unpack_kernel, n_z, shard, bias_lanes),
        out_shape=[
            shape((rows, got.shape[2] - n_z * lanes), BF), shape((n_z, rows + 2 * blocks, lanes), BF),
        ],
        compiler_params=params(),
        cost_estimate=cost(3),
    )(got)


def turn_kernel(n_z, rows, cuts, at_ref, *refs):
    got = refs[:n_z]
    outs, held = refs[n_z:-1], refs[-1]
    for k in range(n_z):
        held[at_ref[0] ^ k] = got[k][...]
    whole = jnp.concatenate([held[z, :rows].astype(F32).T for z in range(n_z)], 1)
    for i, out in enumerate(outs[: len(cuts) - 1]):
        out[...] = whole[cuts[i] : cuts[i + 1]].astype(BF)
    if len(outs) == len(cuts):
        outs[-1][...] = held[:, rows:]


def turn(z_at, got, rows, cuts):
    n_z = len(got)
    outs = [shape((cuts[i + 1] - cuts[i], rows * n_z), BF) for i in range(len(cuts) - 1)]
    if got[0].shape[0] > rows:
        outs.append(shape((n_z, got[0].shape[0] - rows, got[0].shape[1]), BF))
    return pl.pallas_call(
        functools.partial(turn_kernel, n_z, rows, cuts),
        in_specs=[pl.BlockSpec(memory_space=pltpu.SMEM)] + [pl.BlockSpec(memory_space=pltpu.VMEM)] * n_z,
        out_shape=outs,
        scratch_shapes=[pltpu.VMEM((n_z,) + got[0].shape, BF)],
        compiler_params=params(),
        cost_estimate=cost(3),
    )(z_at, *got)


def turn_w_kernel(n_z, at_ref, *refs):
    got, out_got = refs[:n_z], refs[n_z : 2 * n_z]
    w_out, held, out_held = refs[2 * n_z :]
    for k in range(n_z):
        held[at_ref[0] ^ k] = got[k][...]
        out_held[at_ref[0] ^ k] = out_got[k][...]
    columns_part = jnp.concatenate([held[z].astype(F32).T for z in range(n_z)], 1)
    rows = [out_held[z].astype(F32) for z in range(n_z)]
    w_out[...] = jnp.concatenate([columns_part] + rows, 0).astype(BF)


def turn_w(z_at, got, out_got):
    n_z = len(got)
    rows, lanes = got[0].shape
    return pl.pallas_call(
        functools.partial(turn_w_kernel, n_z),
        in_specs=[SMEM] + [pl.BlockSpec(memory_space=pltpu.VMEM)] * (2 * n_z),
        out_shape=shape((lanes + n_z * out_got[0].shape[0], rows * n_z), BF),
        scratch_shapes=[pltpu.VMEM((n_z, rows, lanes), BF), pltpu.VMEM((n_z,) + out_got[0].shape, BF)],
        compiler_params=params(),
        cost_estimate=cost(3),
    )(z_at, *got, *out_got)


def split_kernel(n_z, width, n_in, *refs):
    total = refs[0][...].astype(F32)
    for ref in refs[1:n_in]:
        total = total + ref[...].astype(F32)
    qkv_out, out_out = refs[n_in:]
    model = total.shape[1]
    part = width // n_z
    turned = total[: 3 * width].T
    rows = model // n_z
    bias = total[4 * width : 4 * width + 1]
    for z in range(n_z):
        qkv_out[z] = turned[z * rows : (z + 1) * rows].astype(BF)
        pieces = [total[3 * width + z * part : 3 * width + (z + 1) * part]]
        for i in range(4):
            at = i * width + z * part
            pieces.append(jnp.concatenate([bias[:, at : at + part], jnp.zeros((1, model - part), F32)], 1))
        spare = out_out.shape[1] - part - 4
        if spare:
            pieces.append(jnp.zeros((spare, model), F32))
        out_out[z] = jnp.concatenate(pieces, 0).astype(BF)


def split_parts(values, n_z):
    rows, model = values[0].shape
    width = (rows - 16) // 4
    out_rows = -(-(width // n_z + 4) // 8) * 8
    return pl.pallas_call(
        functools.partial(split_kernel, n_z, width, len(values)),
        out_shape=[shape((n_z, model // n_z, 3 * width), BF), shape((n_z, out_rows, model), BF)],
        compiler_params=params(),
        cost_estimate=cost(3),
    )(*values)


def deal_kernel(n_in, blocks, *refs):
    sums = []
    for i in range(2):
        total = refs[i * n_in][...].astype(F32)
        for ref in refs[i * n_in + 1 : (i + 1) * n_in]:
            total = total + ref[...].astype(F32)
        sums.append(total)
    total = jnp.concatenate(sums, 1)
    rows = total.shape[0] // blocks
    for e in range(blocks):
        refs[2 * n_in][e] = total[e * rows : (e + 1) * rows].astype(BF)


def deal(first, second, blocks):
    rows = first[0].shape[0]
    lanes = first[0].shape[1] + second[0].shape[1]
    return pl.pallas_call(
        functools.partial(deal_kernel, len(first), blocks),
        out_shape=shape((blocks, rows // blocks, lanes), BF),
        compiler_params=params(),
        cost_estimate=cost(3),
    )(*first, *second)


def turn_up_kernel(n_z, at_ref, *refs):
    got, (out, held) = refs[:n_z], refs[n_z:]
    for t in range(n_z):
        total = got[t][0].astype(F32)
        for s in range(1, got[t].shape[0]):
            total = total + got[t][s].astype(F32)
        held[lax.rem(at_ref[0] - t + n_z, n_z)] = total
    turned = jnp.concatenate([held[z].T for z in range(n_z)], 1)
    rows = out.shape[1]
    for z in range(n_z):
        out[z] = turned[z * rows : (z + 1) * rows].astype(BF)


def turn_up(z_at, got):
    n_z = len(got)
    _, ff, model = got[0].shape
    return pl.pallas_call(
        functools.partial(turn_up_kernel, n_z),
        in_specs=[pl.BlockSpec(memory_space=pltpu.SMEM)] + [pl.BlockSpec(memory_space=pltpu.VMEM)] * n_z,
        out_shape=shape((n_z, model // n_z, n_z * ff), BF),
        scratch_shapes=[pltpu.VMEM((n_z, ff, model), F32)],
        compiler_params=params(),
        cost_estimate=cost(3),
    )(z_at, *got)


def columns_kernel(groups, n_in, *refs):
    for out, (source, rows, start, size, count) in zip(refs[n_in:], groups):
        ref = refs[source]
        pieces = []
        for i in range(count):
            for n in range(ref.shape[0]):
                pieces.append(ref[n].astype(F32)[:rows, start + i * size : start + (i + 1) * size])
        out[...] = jnp.concatenate(pieces, 1)


def columns(sources, groups):
    return pl.pallas_call(
        functools.partial(columns_kernel, groups, len(sources)),
        out_shape=[shape((rows, sources[i].shape[0] * size * count), F32) for i, rows, _, size, count in groups],
        compiler_params=params(),
        cost_estimate=cost(3),
    )(*sources)


def mod_columns_kernel(early_ref, late_ref, out):
    shard = out.shape[0]
    pieces = []
    for ref in (early_ref, late_ref):
        for i in range(ref.shape[2] // shard):
            for n in range(ref.shape[0]):
                pieces.append(ref[n].astype(F32)[:shard, i * shard : (i + 1) * shard])
    out[...] = jnp.concatenate(pieces, 1)


def mod_columns(early, late, shard):
    return pl.pallas_call(
        mod_columns_kernel,
        out_shape=[shape((shard, 6 * shard * early.shape[0]), F32)],
        compiler_params=params(),
        cost_estimate=cost(3),
    )(early, late)


def place_kernel(at_ref, *refs):
    out = refs[-1]
    for k, ref in enumerate(refs[:-1]):
        out[at_ref[0] ^ k] = ref[...]


def place(at, got):
    return pl.pallas_call(
        place_kernel,
        in_specs=[pl.BlockSpec(memory_space=pltpu.SMEM)] + [pl.BlockSpec(memory_space=pltpu.VMEM)] * len(got),
        out_shape=shape((len(got),) + got[0].shape, got[0].dtype),
        compiler_params=params(),
        cost_estimate=cost(3),
    )(at, *got)


def attn_fwd_kernel(head_size, h_ref, w_a, w_b, qb_ref, vb_ref, segc_ref, segr_ref, *rest):
    q_out, k_out, v_out, att_out, lse_out = rest[-5:]
    width = qb_ref.shape[-1]
    length = segr_ref.shape[-1]
    model = h_ref.shape[-1]
    h = h_ref[...].reshape(length, model)
    allowed = segc_ref[0] == segr_ref[0]
    scale = head_size ** (-0.5)
    part = q_out.shape[1:]
    for n, w_ref in enumerate((w_a, w_b)):
        qkv = dot_nt(h, w_ref[: 3 * width])
        q = (qkv[:, :width] + qb_ref[n]).astype(BF)
        k = qkv[:, width : 2 * width].astype(BF)
        v = (qkv[:, 2 * width :] + vb_ref[n]).astype(BF)
        q_out[n] = q.reshape(part)
        k_out[n] = k.reshape(part)
        v_out[n] = v.reshape(part)
        pieces = []
        for i in range(width // head_size):
            cut = slice(i * head_size, (i + 1) * head_size)
            score = jnp.where(allowed, dot_nt(k[:, cut], q[:, cut]) * scale, -1e30)
            top = jnp.max(score, 0, keepdims=True)
            prob = jnp.exp(score - top)
            total = jnp.sum(prob, 0, keepdims=True)
            out_t = dot_tn(v[:, cut], prob.astype(BF)) * (1.0 / total)
            pieces.append(out_t.T)
            lse_out[n, 0, i : i + 1, :] = top + jnp.log(total)
        att_out[n] = jnp.concatenate(pieces, -1).astype(BF).reshape(part)


def attn_fwd(hidden, w_a, w_b, query_bias, value_bias, seg_col, seg_row, head_size, wait):
    n_seq, rows, kept_count, model = hidden.shape
    width = query_bias.shape[-1]
    length = n_seq * kept_count
    heads = width // head_size
    token = pl.BlockSpec((n_seq, 1, kept_count, model), lambda r: (0, r, 0, 0))
    part = pl.BlockSpec((2, n_seq, 1, kept_count, width), lambda r: (0, 0, r, 0, 0))
    weight = pl.BlockSpec(w_a.shape, lambda r: (0, 0))
    bias = pl.BlockSpec((2, 1, width), lambda r: (0, 0, 0))
    part_shape = shape((2, n_seq, rows, kept_count, width), BF)
    return pl.pallas_call(
        functools.partial(attn_fwd_kernel, head_size),
        grid=(rows,),
        in_specs=[
            token, weight, weight, bias, bias,
            pl.BlockSpec((1, length, 1), lambda r: (r, 0, 0)),
            pl.BlockSpec((1, 1, length), lambda r: (r, 0, 0)),
        ]
        + [ANY] * len(wait),
        out_specs=[part, part, part, part, pl.BlockSpec((2, 1, heads, length), lambda r: (0, r, 0, 0))],
        out_shape=[part_shape] * 4 + [shape((2, rows, heads, length), F32)],
        compiler_params=params(),
        cost_estimate=cost(12),
    )(hidden, w_a, w_b, query_bias, value_bias, seg_col, seg_row, *wait)


def attn_bwd_kernel(head_size, first, n_wait, h_ref, gb_ref, w_a, w_b, q_ref, k_ref, v_ref, att_ref, lse_ref,
                    bias_ref, segc_ref, segr_ref, *rest):
    g_a, g_b, gh_out, sum_qkv, sum_out, sum_bias = rest[-6:]
    gh_in = None if first else rest[n_wait]
    width = q_ref.shape[-1]
    length = segr_ref.shape[-1]
    model = h_ref.shape[-1]
    row = pl.program_id(0)
    h = h_ref[...].reshape(length, model)
    gb = gb_ref[...].reshape(length, model)
    allowed = segc_ref[0] == segr_ref[0]
    scale = head_size ** (-0.5)
    total = None
    for n, w_ref in enumerate((w_a, w_b)):
        grad_att = dot_nt(gb, w_ref[3 * width :]).astype(BF)
        q = q_ref[n].reshape(length, width)
        k = k_ref[n].reshape(length, width)
        v = v_ref[n].reshape(length, width)
        att = att_ref[n].reshape(length, width)
        gq, gk, gv = [], [], []
        for i in range(width // head_size):
            cut = slice(i * head_size, (i + 1) * head_size)
            score = dot_nt(k[:, cut], q[:, cut]) * scale - lse_ref[n, 0, i : i + 1, :]
            prob = jnp.exp(jnp.where(allowed, score, -1e30))
            grad_prob = dot_nt(v[:, cut], grad_att[:, cut])
            inner = jnp.sum(prob * grad_prob, 0, keepdims=True)
            grad_score = (prob * (grad_prob - inner)).astype(BF)
            gq.append((dot_tn(k[:, cut], grad_score) * scale).T)
            gk.append(dot_nn(grad_score, q[:, cut]) * scale)
            gv.append(dot_nn(prob.astype(BF), grad_att[:, cut]))
        grad_qkv = jnp.concatenate(gq + gk + gv, -1).astype(BF)
        term = dot_nn(grad_qkv, w_ref[: 3 * width])
        total = term if total is None else total + term
        term_qkv = dot_tn(grad_qkv, h)
        term_out = dot_tn(att, gb)
        term_bias = jnp.sum(grad_qkv.astype(F32), 0, keepdims=True)

        @pl.when(row == 0)
        def _():
            sum_qkv[n] = term_qkv
            sum_out[n] = term_out
            sum_bias[n] = term_bias

        @pl.when(row != 0)
        def _():
            sum_qkv[n] += term_qkv
            sum_out[n] += term_out
            sum_bias[n] += term_bias

    if first:
        gh_out[...] = total.reshape(gh_out.shape)
    else:
        gh_out[...] = gh_in[...] + total.reshape(gh_out.shape)

    @pl.when(row == pl.num_programs(0) - 1)
    def _():
        for n, g_ref in enumerate((g_a, g_b)):
            g_ref[: 3 * width] = sum_qkv[n].astype(BF)
            g_ref[3 * width : 4 * width] = sum_out[n].astype(BF)
            biases = jnp.concatenate(
                [sum_bias[n, :, :width], sum_bias[n, :, 2 * width :], bias_ref[n],
                 jnp.zeros((1, model - 4 * width), F32)], -1
            )
            g_ref[4 * width :] = jnp.broadcast_to(biases, (16, model)).astype(BF)


def attn_bwd(hidden, grad_branch, w_a, w_b, saved, bias, seg_col, seg_row, head_size, grad_hidden, wait):
    q, k, v, att, lse = saved
    n_seq, rows, kept_count, model = hidden.shape
    width = q.shape[-1]
    length = n_seq * kept_count
    heads = width // head_size
    first = grad_hidden is None
    token = pl.BlockSpec((n_seq, 1, kept_count, model), lambda r: (0, r, 0, 0))
    part = pl.BlockSpec((2, n_seq, 1, kept_count, width), lambda r: (0, 0, r, 0, 0))
    weight = pl.BlockSpec(w_a.shape, lambda r: (0, 0))
    out = pl.BlockSpec((4 * width + 16, model), lambda r: (0, 0))
    own = [] if first else [grad_hidden]
    return pl.pallas_call(
        functools.partial(attn_bwd_kernel, head_size, first, len(wait)),
        grid=(rows,),
        in_specs=[
            token, token, weight, weight, part, part, part, part,
            pl.BlockSpec((2, 1, heads, length), lambda r: (0, r, 0, 0)),
            pl.BlockSpec((2, 1, 2 * width), lambda r: (0, 0, 0)),
            pl.BlockSpec((1, length, 1), lambda r: (r, 0, 0)),
            pl.BlockSpec((1, 1, length), lambda r: (r, 0, 0)),
        ]
        + [ANY] * len(wait)
        + [token] * len(own),
        out_specs=[out, out, token],
        scratch_shapes=[
            pltpu.VMEM((2, 3 * width, model), F32),
            pltpu.VMEM((2, width, model), F32),
            pltpu.VMEM((2, 1, 3 * width), F32),
        ],
        out_shape=[shape((4 * width + 16, model), BF)] * 2 + [shape(hidden.shape, F32)],
        input_output_aliases={} if first else {12 + len(wait): 2},
        compiler_params=params(),
        cost_estimate=cost(24),
    )(hidden, grad_branch, w_a, w_b, q, k, v, att, lse, bias, seg_col, seg_row, *wait, *own)


def pick_slot(table_ref, ends, seg, index):
    first, last = ends
    low = table_ref[0, first, index : index + 1, :]
    return jnp.where(seg == last, table_ref[0, last, index : index + 1, :], low)


def add_slots(out_ref, ends, seg, values, start):
    first, last = ends

    @pl.when(start)
    def _():
        out_ref[...] = jnp.zeros_like(out_ref)

    @pl.when(first == last)
    def _():
        for index, value in enumerate(values):
            out_ref[0, first, index : index + 1] += jnp.sum(value, 0, keepdims=True)

    @pl.when(first != last)
    def _():
        for index, value in enumerate(values):
            out_ref[0, first, index : index + 1] += jnp.sum(jnp.where(seg == first, value, 0.0), 0, keepdims=True)
            out_ref[0, last, index : index + 1] += jnp.sum(jnp.where(seg == last, value, 0.0), 0, keepdims=True)


def ends_of(ends_ref):
    row, part = pl.program_id(0), pl.program_id(1)
    return ends_ref[0, part, row], ends_ref[1, part, row]


def before_attn_kernel(ends_ref, x_ref, seg_ref, table_ref, out_ref):
    ends, seg = ends_of(ends_ref), seg_ref[0, 0]
    normed, _ = normalize(x_ref[0, 0].astype(F32))
    out_ref[0, 0] = (normed * (1.0 + pick_slot(table_ref, ends, seg, 1)) + pick_slot(table_ref, ends, seg, 0)).astype(BF)


def before_attn(ends, inputs, seg, table):
    n_seq, rows, kept_count, model = inputs.shape
    slots = table.shape[1]
    token = pl.BlockSpec((1, 1, kept_count, model), lambda r, j: (j, r, 0, 0))
    return pl.pallas_call(
        before_attn_kernel,
        grid=(rows, n_seq),
        in_specs=[
            SMEM, token,
            pl.BlockSpec((1, 1, kept_count, 1), lambda r, j: (j, r, 0, 0)),
            pl.BlockSpec((1, slots, 6, model), lambda r, j: (r, 0, 0, 0)),
        ],
        out_specs=token,
        out_shape=shape(inputs.shape, BF),
        compiler_params=params(),
        cost_estimate=cost(5),
    )(ends, inputs, seg, table)


def after_attn_kernel(n_seq, width, out_at, ends_ref, x_ref, seg_ref, table_ref, ob_ref, *rest):
    att_refs, w_refs = rest[:n_seq], rest[n_seq : 3 * n_seq]
    br_out, mid_out, h2_out = rest[-3:]
    kept_count, model = x_ref.shape[2:]
    ends, seg = ends_of(ends_ref), seg_ref[0, 0]
    branch = ob_ref[...]
    for j in range(n_seq):
        for n in range(2):
            w = w_refs[j + n * n_seq][pl.ds(out_at, width)]
            branch = branch + dot_nn(att_refs[j][n].reshape(kept_count, width), w)
    mid = x_ref[0, 0].astype(F32) + pick_slot(table_ref, ends, seg, 2) * branch
    normed, _ = normalize(mid)
    br_out[0, 0] = branch
    mid_out[0, 0] = mid
    h2_out[0, 0] = (normed * (1.0 + pick_slot(table_ref, ends, seg, 4)) + pick_slot(table_ref, ends, seg, 3)).astype(BF)


def after_attn(ends, inputs, seg, table, out_bias, weights, atts):
    n_seq, rows, kept_count, model = inputs.shape
    width = atts[0].shape[-1]
    slots = table.shape[1]
    token = pl.BlockSpec((1, 1, kept_count, model), lambda r, j: (j, r, 0, 0))
    part = pl.BlockSpec((2, 1, 1, kept_count, width), lambda r, j: (0, j, r, 0, 0))
    if width % 16 == 0:
        weight, out_at = pl.BlockSpec((width, model), lambda r, j: (3, 0)), 0
    else:
        weight, out_at = pl.BlockSpec((4 * width, model), lambda r, j: (0, 0)), 3 * width
    return pl.pallas_call(
        functools.partial(after_attn_kernel, n_seq, width, out_at),
        grid=(rows, n_seq),
        in_specs=[
            SMEM, token,
            pl.BlockSpec((1, 1, kept_count, 1), lambda r, j: (j, r, 0, 0)),
            pl.BlockSpec((1, slots, 6, model), lambda r, j: (r, 0, 0, 0)),
            pl.BlockSpec((1, model), lambda r, j: (0, 0)),
        ]
        + [part] * len(atts)
        + [weight] * len(weights),
        out_specs=[token] * 3,
        out_shape=[shape(inputs.shape, F32), shape(inputs.shape, F32), shape(inputs.shape, BF)],
        compiler_params=params(),
        cost_estimate=cost(11),
    )(ends, inputs, seg, table, out_bias, *atts, *weights)


def after_mlp_kernel(ends_ref, mid_ref, mlp_ref, gh_ref, br_ref, ct_ref, seg_ref, table_ref, db_ref, *rest):
    res_out, gm_out, gb_out, sums_out, obias_out = rest[-5:]
    ends, seg = ends_of(ends_ref), seg_ref[0, 0]
    step = pl.program_id(1)
    mid = mid_ref[0, 0]
    branch_mlp = mlp_ref[0, 0] + db_ref[...]
    grad_hidden = gh_ref[0, 0]
    grad_result = ct_ref[0, 0].astype(F32)
    res_out[0, 0] = (mid + pick_slot(table_ref, ends, seg, 5) * branch_mlp).astype(BF)
    normed, inv = normalize(mid)
    grad_mid = grad_result + norm_back(grad_hidden * (1.0 + pick_slot(table_ref, ends, seg, 4)), normed, inv)
    gm_out[0, 0] = grad_mid
    grad_branch = (grad_mid * pick_slot(table_ref, ends, seg, 2)).astype(BF)
    gb_out[0, 0] = grad_branch
    values = [grad_mid * br_ref[0, 0], grad_hidden, grad_hidden * normed, grad_result * branch_mlp]
    add_slots(sums_out, ends, seg, values, step == 0)
    start = jnp.logical_and(step == 0, pl.program_id(0) == 0)
    part = jnp.sum(grad_branch.astype(F32), 0, keepdims=True)
    obias_out[...] = jnp.where(start, 0.0, obias_out[...]) + part


def after_mlp(ends, mid, mlp, grad_hidden, branch, cotangent, seg, table, down_bias, wait):
    n_seq, rows, kept_count, model = mid.shape
    slots = table.shape[1]
    token = pl.BlockSpec((1, 1, kept_count, model), lambda r, j: (j, r, 0, 0))
    vector = pl.BlockSpec((1, model), lambda r, j: (0, 0))
    return pl.pallas_call(
        after_mlp_kernel,
        grid=(rows, n_seq),
        in_specs=[
            SMEM, token, token, token, token, token,
            pl.BlockSpec((1, 1, kept_count, 1), lambda r, j: (j, r, 0, 0)),
            pl.BlockSpec((1, slots, 6, model), lambda r, j: (r, 0, 0, 0)),
            vector,
        ]
        + [ANY] * len(wait),
        out_specs=[
            token, token, token,
            pl.BlockSpec((1, slots, 4, model), lambda r, j: (r, 0, 0, 0)),
            vector,
        ],
        out_shape=[
            shape(mid.shape, BF), shape(mid.shape, F32), shape(mid.shape, BF),
            shape((rows, slots, 4, model), F32), shape((1, model), F32),
        ],
        compiler_params=params(),
        cost_estimate=cost(13),
    )(ends, mid, mlp, grad_hidden, branch, cotangent, seg, table, down_bias, *wait)


def last_kernel(ends_ref, x_ref, gh_ref, gm_ref, seg_ref, table_ref, *rest):
    gx_out, sums_out = rest[-2:]
    ends, seg = ends_of(ends_ref), seg_ref[0, 0]
    grad_hidden = gh_ref[0, 0]
    normed, inv = normalize(x_ref[0, 0].astype(F32))
    back = norm_back(grad_hidden * (1.0 + pick_slot(table_ref, ends, seg, 1)), normed, inv)
    gx_out[0, 0] = (gm_ref[0, 0] + back).astype(BF)
    add_slots(sums_out, ends, seg, [grad_hidden, grad_hidden * normed], pl.program_id(1) == 0)


def last_step(ends, inputs, grad_hidden, grad_mid, seg, table, wait):
    n_seq, rows, kept_count, model = inputs.shape
    slots = table.shape[1]
    token = pl.BlockSpec((1, 1, kept_count, model), lambda r, j: (j, r, 0, 0))
    return pl.pallas_call(
        last_kernel,
        grid=(rows, n_seq),
        in_specs=[
            SMEM, token, token, token,
            pl.BlockSpec((1, 1, kept_count, 1), lambda r, j: (j, r, 0, 0)),
            pl.BlockSpec((1, slots, 6, model), lambda r, j: (r, 0, 0, 0)),
        ]
        + [ANY] * len(wait),
        out_specs=[token, pl.BlockSpec((1, slots, 2, model), lambda r, j: (r, 0, 0, 0))],
        out_shape=[shape(inputs.shape, BF), shape((rows, slots, 2, model), F32)],
        compiler_params=params(),
        cost_estimate=cost(8),
    )(ends, inputs, grad_hidden, grad_mid, seg, table, *wait)


def mlp_kernel(n_up, n_down, first, n_wait, h_ref, gm_ref, ub_ref, *rest):
    up_refs = rest[:n_up]
    down_refs = rest[n_up : n_up + n_down]
    if first:
        mlp_in = gh_in = None
    else:
        mlp_in, gh_in = rest[n_up + n_down + n_wait : n_up + n_down + n_wait + 2]
    mlp_out, gh_out, own_out, other_out, gub_out, up, down, sum_up, sum_down, sum_bias = rest[-10:]
    step = pl.program_id(0)
    model = h_ref.shape[-1]

    @pl.when(step == 0)
    def _():
        for refs, whole in ((up_refs, up), (down_refs, down)):
            at = 0
            for ref in refs:
                block = ref[...].reshape(-1, model)
                whole[at : at + block.shape[0]] = block
                at += block.shape[0]

    h = h_ref[...]
    gm = gm_ref[...]
    pre = dot_nt(h, up[...]) + ub_ref[0]
    square = pre * pre
    tanh_part = jnp.tanh(GELU_C * pre * (1.0 + GELU_A * square))
    half = 0.5 * (1.0 + tanh_part)
    activated = (pre * half).astype(BF)
    slope = half + 0.5 * pre * (1.0 - tanh_part * tanh_part) * GELU_C * (1.0 + 3.0 * GELU_A * square)
    grad_pre = (dot_nt(gm, down[...]) * slope).astype(BF)
    mlp_term = dot_nn(activated, down[...])
    gh_term = dot_nn(grad_pre, up[...])
    mlp_out[...] = mlp_term if first else mlp_in[...] + mlp_term
    gh_out[...] = gh_term if first else gh_in[...] + gh_term
    up_term = dot_tn(grad_pre, h)
    down_term = dot_tn(activated, gm)
    bias_term = jnp.sum(grad_pre.astype(F32), 0, keepdims=True)

    @pl.when(step == 0)
    def _():
        sum_up[...] = up_term
        sum_down[...] = down_term
        sum_bias[...] = bias_term

    @pl.when(step != 0)
    def _():
        sum_up[...] += up_term
        sum_down[...] += down_term
        sum_bias[...] += bias_term

    @pl.when(step == pl.num_programs(0) - 1)
    def _():
        half_rows = sum_up.shape[0] // 2
        own_out[0] = sum_up[:half_rows].astype(BF)
        own_out[1] = sum_down[:half_rows].astype(BF)
        other_out[0] = sum_up[half_rows:].astype(BF)
        other_out[1] = sum_down[half_rows:].astype(BF)
        gub_out[...] = sum_bias[...]


def mlp_step(hidden, grad_mlp, up_bias, ups, downs, sums, wait):
    count, model = hidden.shape
    chunk = min(1024, count)
    width = sum(u.shape[0] * u.shape[1] for u in ups)
    first = sums is None
    own = [] if first else list(sums)
    token = pl.BlockSpec((chunk, model), lambda i: (i, 0))
    weights = [pl.BlockSpec(u.shape, lambda i: (0, 0, 0)) for u in ups + downs]
    grads = pl.BlockSpec((2, width // 2, model), lambda i: (0, 0, 0))
    inputs = 3 + len(ups) + len(downs) + len(wait)
    return pl.pallas_call(
        functools.partial(mlp_kernel, len(ups), len(downs), first, len(wait)),
        grid=(count // chunk,),
        in_specs=[token, token, pl.BlockSpec((1, 1, width), lambda i: (0, 0, 0))]
        + weights
        + [ANY] * len(wait)
        + [token] * len(own),
        out_specs=[token, token, grads, grads, pl.BlockSpec((1, width), lambda i: (0, 0))],
        out_shape=[
            shape((count, model), F32), shape((count, model), F32),
            shape((2, width // 2, model), BF), shape((2, width // 2, model), BF), shape((1, width), F32),
        ],
        scratch_shapes=[
            pltpu.VMEM((width, model), BF), pltpu.VMEM((width, model), BF),
            pltpu.VMEM((width, model), F32), pltpu.VMEM((width, model), F32), pltpu.VMEM((1, width), F32),
        ],
        input_output_aliases={} if first else {inputs: 0, inputs + 1: 1},
        compiler_params=params(),
        cost_estimate=cost(32),
    )(hidden, grad_mlp, up_bias, *ups, *downs, *wait, *own)


def tie(value, *after):
    return lax.optimization_barrier((value,) + after)[0]


def body(
    n_z, n_seq,
    tokens, conditioning, segments, kept, cotangent,
    mod_weight, mod_bias, qkv_weight, query_bias, value_bias, out_weight, out_bias,
    up_weight, up_bias, down_weight, down_bias,
):
    row_count, seq_tokens, model = tokens.shape
    kept_count = kept.shape[1]
    slots = conditioning.shape[1]
    head_size = model // HEADS
    rows = row_count // n_seq
    shard = qkv_weight.shape[0]
    blocks = 2 * n_seq
    devices = n_z * blocks
    width = model // blocks
    part = width // n_z
    flat = n_seq * rows * kept_count
    ff_shard = down_weight.shape[0]
    z_at = lax.axis_index("z")
    core_at = lax.axis_index("core")
    seq_at = lax.axis_index("seq")
    block_at = core_at * n_seq + seq_at
    relative = block_at ^ jnp.arange(blocks)
    z_relative = z_at ^ jnp.arange(n_z)
    seq_relative = seq_at ^ jnp.arange(n_seq)
    core_relative = core_at ^ jnp.arange(2)
    z_ring = (z_at - jnp.arange(n_z)) % n_z
    seq_scalar = seq_at.reshape(1).astype(jnp.int32)
    z_scalar = z_at.reshape(1).astype(jnp.int32)
    mod_shard = 6 * shard

    def over_core(value):
        return lax.ppermute(value, "core", [(0, 1), (1, 0)])

    def over_seq(value, by):
        return lax.ppermute(value, "seq", [(i, i ^ by) for i in range(n_seq)])

    def over_z(value, by):
        return lax.ppermute(value, "z", [(i, i ^ by) for i in range(n_z)])

    def shift_z(value, by):
        return lax.ppermute(value, "z", [(i, (i + by) % n_z) for i in range(n_z)])

    def all_to_all(value):
        return lax.all_to_all(value, EVERY, 0, 0, tiled=True)

    def dense_to_all(value):
        return lax.all_to_all(value, DENSE, 0, 0, tiled=True)

    def to_z(value):
        mine = [lax.dynamic_index_in_dim(value, z_at ^ k, 0, keepdims=False) for k in range(n_z)]
        return [mine[0]] + [over_z(mine[k], k) for k in range(1, n_z)]

    def sum_of(values):
        total = values[0].astype(F32)
        for value in values[1:]:
            total = total + value.astype(F32)
        return total

    def plane(value):
        return [value] + [over_seq(value, j) for j in range(1, n_seq)]

    def seq_to_all(value):
        return lax.all_to_all(value, "seq", 0, 0, tiled=True)

    def gather_seq(value):
        return seq_to_all(jnp.broadcast_to(value[None], (n_seq,) + value.shape))

    def to_rows(value):
        return seq_to_all(value.reshape((n_seq, rows) + value.shape[1:]))

    def from_rows(value):
        return seq_to_all(value).reshape((row_count,) + value.shape[2:])

    first_cols = pack(
        n_z, blocks, qkv_weight, mod_weight, up_weight, (mod_bias, query_bias, value_bias, out_bias, up_bias, down_bias)
    )
    first_got = dense_to_all(first_cols)
    spread_out = []
    for d in range(devices):
        z, c, s = d % n_z, (d // n_z) // n_seq, (d // n_z) % n_seq
        spread_out.append((d, (z * 2 + c) * n_seq + s))
    down_got = plane(tie(down_weight, first_cols))
    out_part = lax.ppermute(tie(out_weight, first_cols), EVERY, spread_out)
    out_got = [out_part] + [over_z(out_part, k) for k in range(1, n_z)]

    places = jnp.arange(seq_tokens, dtype=jnp.int32)
    kept = tie(kept, first_cols)
    hits = kept[:, :, None] == places
    pick = hits.astype(BF)
    kept_here = jnp.any(hits, 1)

    def pick_kept(value):
        return jnp.einsum("rkt,rtd->rkd", pick, value, preferred_element_type=F32).astype(BF)

    def put_kept(value, base):
        spread = jnp.einsum("rkt,rkd->rtd", pick, value, preferred_element_type=F32).astype(BF)
        return jnp.where(kept_here[:, :, None], spread, base)

    picked = pick_kept(tokens)
    picked_ct = pick_kept(cotangent)
    inputs = to_rows(tie(picked, first_got))

    cond_float = conditioning.astype(F32).reshape(row_count * slots, model)
    cond_act = (cond_float / (1.0 + jnp.exp(-cond_float))).astype(BF)
    act_other = over_core(cond_act)
    act_pair = jnp.concatenate([jnp.where(core_at == 0, cond_act, act_other), jnp.where(core_at == 0, act_other, cond_act)])
    act_got = [act_pair] + [over_z(act_pair, k) for k in range(1, n_z)]
    act_all = jnp.take(jnp.stack(act_got), z_relative, axis=0).reshape(-1, model)

    numbers = jnp.arange(slots, dtype=jnp.int32)
    query_seg = jnp.sum(jnp.where(hits, segments[:, None, :], 0), -1)
    kept_hits = jnp.sum((query_seg[:, :, None] == numbers).astype(jnp.int32), 1)
    all_hits = jnp.sum((segments[:, :, None] == numbers).astype(jnp.int32), 1)
    small = jnp.concatenate([query_seg, kept_hits, all_hits - kept_hits], -1)
    small_got = plane(small)
    small = jnp.take(jnp.stack(small_got), seq_relative, axis=0)
    sample_counts = jnp.sum(small[:, :, kept_count:], 0).reshape(row_count, 2, slots).transpose(0, 2, 1)
    seg = lax.dynamic_slice_in_dim(small[:, :, :kept_count], seq_at * rows, rows, 1)
    seg_rows = seg.transpose(1, 0, 2).reshape(rows, 1, n_seq * kept_count)
    seg_cols = seg_rows.reshape(rows, n_seq * kept_count, 1)
    seg_tokens = seg.reshape(n_seq, rows, kept_count, 1)
    ends = jnp.stack([seg[:, :, 0], seg[:, :, -1]])

    qkv_rows, z_cols = unpack(tie(first_got, *act_got[1:], *small_got[1:], *out_got[1:], *down_got[1:], picked), n_z, shard, mod_shard + ff_shard, mod_shard + ff_shard + 4 * shard)
    qkv_got = [qkv_rows] + [over_z(qkv_rows, k) for k in range(1, n_z)]
    w_own = turn_w(z_scalar, qkv_got, out_got)
    z_got = to_z(tie(z_cols, *qkv_got[1:]))
    mod_cols, up_part, bias_got = turn(tie(z_scalar, w_own), z_got, blocks * shard, (0, mod_shard, mod_shard + ff_shard))
    bias_got = bias_got.astype(F32)
    mod_b = bias_got[:, :blocks, :mod_shard].reshape(-1)
    up_b = bias_got[:, :blocks, mod_shard:].reshape(-1)
    query_b, value_b, out_b, down_b = [
        bias_got[:, blocks:, i * shard : (i + 1) * shard].reshape(-1) for i in range(4)
    ]

    mod_part = tie(dot_nt(act_all, mod_cols), inputs).reshape(devices, rows * slots, mod_shard)
    modulation = tie(all_to_all(mod_part), picked_ct).transpose(1, 0, 2).reshape(rows * slots, 6 * model) + mod_b
    table = modulation.reshape(rows, slots, 6, model)

    def token_mod(index):
        value = table[None, :, None, 0, index]
        for slot in range(1, slots):
            value = jnp.where(seg_tokens == slot, table[None, :, None, slot, index], value)
        return value

    hidden_one = before_attn(ends, inputs, seg_tokens, table)

    w_all = plane(w_own)
    w_all = w_all + [over_core(w) for w in w_all]

    down_ring = [place(seq_scalar, down_got)]
    up_ring = [gather_seq(tie(up_part, hidden_one))]
    down_ring.append(shift_z(tie(down_ring[0], *z_got[1:]), 1))
    for t in range(2, n_z):
        if t == 2:
            down_ring.append(shift_z(tie(down_ring[1], hidden_one), 1))
            up_ring.append(shift_z(tie(up_ring[0], down_ring[2]), 1))
        else:
            down_ring.append(shift_z(tie(down_ring[-1], up_ring[-1]), 1))
        up_ring.append(shift_z(tie(up_ring[-1], down_ring[-1]) if t > 2 else up_ring[-1], 1))
    while len(up_ring) < n_z:
        up_ring.append(shift_z(up_ring[-1], 1))
    down_other = [over_core(value) for value in down_ring]
    up_other = [over_core(value) for value in up_ring]

    def by_block(value):
        return jnp.take(value.reshape(blocks, 1, width), relative, axis=0)

    query_b, value_b = by_block(query_b), by_block(value_b)
    up_b = jnp.take(up_b.reshape(n_z, 2, n_seq * ff_shard), core_relative, axis=1)
    up_b = jnp.take(up_b, z_ring, axis=0).reshape(n_z, 1, blocks * ff_shard)

    def pair(value, j):
        return jnp.stack([value[j], value[j + n_seq]])

    saved = []
    for j in range(n_seq):
        saved.append(attn_fwd(
            hidden_one, w_all[j], w_all[j + n_seq], pair(query_b, j), pair(value_b, j), seg_cols, seg_rows, head_size, [],
        ))
    branch_attn, mid, hidden_two = after_attn(
        ends, inputs, seg_tokens, table, out_b.reshape(1, -1), w_all, [s[3] for s in saved],
    )
    grad_result = to_rows(tie(picked_ct, up_ring[0]))
    grad_mlp = (grad_result.astype(F32) * token_mod(5)).astype(BF)
    grad_down_bias = jnp.sum(grad_mlp.astype(F32), (0, 1, 2))

    order = list(range(n_z))
    hidden_flat = hidden_two.reshape(flat, model)
    grad_flat = grad_mlp.reshape(flat, model)
    sums = None
    cores, sends, planes, down_sums, grad_up_bias = [], [], [], {}, {}
    ring = []
    for at, t in enumerate(order):
        ups = [up_ring[t], up_other[t]]
        downs = [down_ring[t], down_other[t]]
        if ff_shard % 16:
            ups = [jnp.concatenate([u.reshape(-1, model) for u in ups])[None]]
            downs = [jnp.concatenate([d.reshape(-1, model) for d in downs])[None]]
        wait = []
        if at >= 2:
            wait.extend(sends[at - 2])
        if at >= 3:
            wait.append(planes[at - 3])
        mlp_sum, gh_sum, own, other, grad_up_bias[t] = mlp_step(
            hidden_flat, grad_flat, up_b[t : t + 1], ups, downs, sums, wait
        )
        sums = (mlp_sum, gh_sum)
        cores.append(over_core(other))
        both = (own.astype(F32) + cores[at].astype(F32)).reshape(2, n_seq, ff_shard, model)
        sends.append([both[0].astype(BF)])
        planes.append(seq_to_all(sends[at][0]))
        down_sums[t] = both[1]
        if t and len(ring) == t - 1:
            value = both[1] if t == 1 else both[1] + ring[-1].astype(F32)
            sends[at].append(value.astype(BF))
            ring.append(shift_z(sends[at][1], 1))

    last = n_z - 1
    res, grad_mid, grad_branch, sums_late, grad_out_bias = after_mlp(
        ends, mid, sums[0].reshape(mid.shape), sums[1].reshape(mid.shape), branch_attn, grad_result, seg_tokens, table,
        down_b.reshape(1, -1), sends[last - 1] + [planes[last - 2]],
    )

    def natural_block(value):
        return by_block(value.reshape(-1))

    late_bias = jnp.concatenate([natural_block(grad_out_bias), natural_block(grad_down_bias)], -1)
    late = sums_late.reshape(rows * slots, 4, devices, shard).transpose(2, 0, 1, 3).reshape(devices, rows * slots, -1)
    late = late.astype(BF)
    waits = sends[last] + [planes[last - 1]]
    grad_hidden = None
    w_cores, w_values, w_planes = [], [], []
    for at, j in enumerate([n_seq - 1] + list(range(1, n_seq - 1)) + [0]):
        g_own, g_other, grad_hidden = attn_bwd(
            hidden_one, grad_branch, w_all[j], w_all[j + n_seq], saved[j],
            pair(late_bias, j), seg_cols, seg_rows, head_size, grad_hidden, waits,
        )
        waits = []
        if at == 0:
            waits = [planes[last]]
            late = all_to_all(tie(late, g_own)).reshape(-1, 4 * shard)
            res = tie(res, g_own)
            res_mine = [lax.dynamic_index_in_dim(res, seq_at ^ k, 0, keepdims=False) for k in range(n_seq)]
            res_got = [res_mine[0]] + [over_seq(res_mine[k], k) for k in range(1, n_seq)]
            down_last = (down_sums[0] + ring[-1].astype(F32)).astype(BF)
        elif at == 1:
            late_mod = dot_tn(act_all, tie(late, g_own)).astype(BF).reshape(devices, shard, 4 * shard)
            natural = jnp.stack([grad_up_bias[t] for t in range(n_z)]).reshape(n_z, 2, n_seq * ff_shard)
            natural = jnp.take(jnp.take(natural, core_relative, axis=1), z_ring, axis=0).reshape(devices, 1, ff_shard)
            late_got = all_to_all(jnp.concatenate([late_mod, natural.astype(BF)], 1))
            up_bias_grad = jnp.sum(late_got[:, shard].astype(F32), 0)
            up_turned = turn_up(z_scalar, [planes[order.index(t)] for t in range(n_z)])
            up_parts = to_z(up_turned)
            waits = [ring[-1], late, up_turned] + res_got[1:]
        elif at == 2:
            waits = [late_got]
            down_parts = seq_to_all(tie(down_last, g_own))
            down_grad = jnp.sum(down_parts.astype(F32), 0)
        elif at == 3:
            waits = [down_parts] + up_parts[1:]
        w_cores.append(over_core(g_other))
        w_values.append((g_own.astype(F32) + w_cores[at].astype(F32)).astype(BF))
        w_planes.append(over_seq(w_values[at], j) if j else w_values[at])
        if at >= 1:
            waits.append(w_values[at - 1])
        if at == n_seq - 2:
            waits.append(w_values[at])

    grad_x, sums_early = last_step(ends, inputs, grad_hidden, grad_mid, seg_tokens, table, waits)
    grad_mine = [lax.dynamic_index_in_dim(grad_x, seq_at ^ k, 0, keepdims=False) for k in range(n_seq)]
    grad_got = [grad_mine[0]] + [over_seq(grad_mine[k], k) for k in range(1, n_seq)]

    def in_place(got):
        return place(seq_scalar, got).reshape((row_count,) + got[0].shape[1:])

    res_got[0] = tie(res_got[0], grad_x)
    output = put_kept(in_place(res_got), tokens)
    tokens_grad = put_kept(in_place(grad_got), cotangent)

    qkv_parts, out_parts = split_parts(w_planes, n_z)
    qkv_parts = to_z(qkv_parts)
    out_parts = to_z(out_parts)
    back_out = lax.ppermute(sum_of(out_parts).astype(BF), EVERY, [(t, d) for d, t in spread_out]).astype(F32)
    out_grad = back_out[:part]
    small_grads = back_out[part : part + 4, :part]

    early = sums_early.reshape(rows * slots, 2, devices, shard).transpose(2, 0, 1, 3).reshape(devices, rows * slots, -1)
    early = all_to_all(early.astype(BF)).reshape(-1, 2 * shard)
    early_mod = dot_tn(act_all, early).astype(BF).reshape(devices, shard, 2 * shard)
    mod_sums = jnp.concatenate([jnp.sum(sums_early, (0, 1)), jnp.sum(sums_late, (0, 1))]).reshape(devices, 6 * shard)
    mod_sums = mod_sums.astype(BF).reshape(devices, 3, 2 * shard)
    mod_got = all_to_all(jnp.concatenate([early_mod, mod_sums], 1))
    mod_bias_grad = jnp.sum(mod_got[:, shard:].reshape(devices, -1).astype(F32), 0)
    dense_got = dense_to_all(deal(qkv_parts, up_parts, blocks))
    qkv_grad, up_grad = columns(
        [dense_got], [(0, shard, 0, width, 3), (0, shard, 3 * width, ff_shard, n_z)]
    )
    (mod_grad,) = mod_columns(mod_got, late_got, shard)
    return (
        output, tokens_grad, mod_grad, mod_bias_grad, qkv_grad, small_grads[0], small_grads[1],
        out_grad, small_grads[2], up_grad, up_bias_grad, down_grad, small_grads[3], sample_counts,
    )


def solution(mesh):
    n_batch, n_seq = mesh.shape["batch"], mesh.shape["seq"]
    split = Mesh(mesh.devices.reshape(n_batch // 2, 2, n_seq), ("z", "core", "seq"))
    batch = ("z", "core")
    both = ("z", "core", "seq")
    row_split = P(batch, "seq", None)
    matrix = P(both, None)
    vector = P(both)
    return jax.shard_map(
        functools.partial(body, n_batch // 2, n_seq),
        mesh=split,
        in_specs=(
            row_split, P(batch, None, None), P(batch, "seq"), P(batch, "seq"), row_split,
            matrix, vector, matrix, vector, vector, matrix, vector, matrix, vector, matrix, vector,
        ),
        out_specs=(
            row_split, row_split, matrix, vector, matrix, vector, vector,
            matrix, vector, matrix, vector, matrix, vector, P(batch, None, None),
        ),
        check_vma=False,
    )
```

```python
import functools

import jax
import jax.numpy as jnp
from jax import lax
from jax.experimental import pallas as pl
from jax.experimental.pallas import tpu as pltpu
from jax.sharding import Mesh
from jax.sharding import PartitionSpec as P

HEADS = 16
EPS = 1e-06
GELU_C = 0.7978845608028654
GELU_A = 0.044715
BF = jnp.bfloat16
F32 = jnp.float32
VMEM = 58 * 1024 * 1024
ANY = pl.BlockSpec(memory_space=pl.ANY)
SMEM = pl.BlockSpec(memory_space=pltpu.SMEM)
EVERY = ("z", "core", "seq")
DENSE = ("core", "seq")


def normalize(values):
    center = values - jnp.mean(values, -1, keepdims=True)
    scale_inv = lax.rsqrt(jnp.mean(center * center, -1, keepdims=True) + EPS)
    return (center * scale_inv, scale_inv)


def norm_back(grad_norm, normed, scale_inv):
    return scale_inv * (
        grad_norm
        - jnp.mean(grad_norm, -1, keepdims=True)
        - normed * jnp.mean(grad_norm * normed, -1, keepdims=True)
    )


def dot_nn(a, b):
    return lax.dot_general(a, b, (((1,), (0,)), ((), ())), preferred_element_type=F32)


def dot_nt(a, b):
    return lax.dot_general(a, b, (((1,), (1,)), ((), ())), preferred_element_type=F32)


def dot_tn(a, b):
    return lax.dot_general(a, b, (((0,), (0,)), ((), ())), preferred_element_type=F32)


def params():
    return pltpu.CompilerParams(vmem_limit_bytes=VMEM)


def cost(micros):
    return pl.CostEstimate(flops=int(micros * 1.15e9), bytes_accessed=0, transcendentals=0)


def shape(dims, kind):
    return jax.ShapeDtypeStruct(tuple(dims), kind)


def pack_kernel(n_z, blocks, qkv_ref, mod_ref, up_ref, mb_ref, qb_ref, vb_ref, ob_ref, ub_ref, db_ref, out_ref):
    shard, model3 = qkv_ref.shape
    model = model3 // 3
    width = model // blocks
    devices = n_z * blocks
    ff_shard = up_ref.shape[1] // devices
    mod_shard = mod_ref.shape[1] // devices
    lanes = out_ref.shape[2]
    qkv = qkv_ref[...].astype(F32)
    mod = mod_ref[...].astype(F32)
    up = up_ref[...].astype(F32)
    tail = [r[...].astype(F32) for r in (mb_ref, ub_ref, qb_ref, vb_ref, ob_ref, db_ref)]
    tail.append(jnp.zeros((1, lanes - sum(r.shape[1] for r in tail)), F32))
    tail = [jnp.concatenate(tail, 1)]
    spare = out_ref.shape[1] - shard - 1
    if spare:
        tail.append(jnp.zeros((spare, lanes), F32))
    for e in range(blocks):
        pieces = []
        for z in range(n_z):
            d = z * blocks + e
            pieces.append(mod[:, d * mod_shard : (d + 1) * mod_shard])
            pieces.append(up[:, d * ff_shard : (d + 1) * ff_shard])
        for i in range(3):
            pieces.append(qkv[:, i * model + e * width : i * model + (e + 1) * width])
        out_ref[e] = jnp.concatenate([jnp.concatenate(pieces, 1)] + tail, 0).astype(BF)


def pack(n_z, blocks, qkv, mod, up, biases):
    shard = qkv.shape[0]
    lanes = (qkv.shape[1] + mod.shape[1] + up.shape[1]) // blocks
    rows = -(-(shard + 1) // 8) * 8
    return pl.pallas_call(
        functools.partial(pack_kernel, n_z, blocks),
        out_shape=shape((blocks, rows, lanes), BF),
        compiler_params=params(),
        cost_estimate=cost(3),
    )(qkv, mod, up, *[b.reshape(1, -1) for b in biases])


def unpack_kernel(n_z, shard, bias_lanes, got_ref, qkv_out, z_out):
    blocks = got_ref.shape[0]
    lanes = z_out.shape[2]
    got = [got_ref[e].astype(F32) for e in range(blocks)]
    whole = jnp.concatenate([g[:shard] for g in got], 0)
    qkv_out[...] = whole[:, n_z * lanes :].astype(BF)
    rows = [g[shard : shard + 1, :lanes] for g in got]
    rest = bias_lanes - lanes
    rows += [jnp.concatenate([g[shard : shard + 1, lanes:bias_lanes], jnp.zeros((1, lanes - rest), F32)], 1) for g in got]
    for z in range(n_z):
        z_out[z] = jnp.concatenate([whole[:, z * lanes : (z + 1) * lanes]] + rows, 0).astype(BF)


def unpack(got, n_z, shard, lanes, bias_lanes):
    blocks = got.shape[0]
    rows = blocks * shard
    return pl.pallas_call(
        functools.partial(unpack_kernel, n_z, shard, bias_lanes),
        out_shape=[
            shape((rows, got.shape[2] - n_z * lanes), BF), shape((n_z, rows + 2 * blocks, lanes), BF),
        ],
        compiler_params=params(),
        cost_estimate=cost(3),
    )(got)


def turn_kernel(n_z, rows, cuts, at_ref, *refs):
    got = refs[:n_z]
    outs, held = refs[n_z:-1], refs[-1]
    for k in range(n_z):
        held[at_ref[0] ^ k] = got[k][...]
    whole = jnp.concatenate([held[z, :rows].astype(F32).T for z in range(n_z)], 1)
    for i, out in enumerate(outs[: len(cuts) - 1]):
        out[...] = whole[cuts[i] : cuts[i + 1]].astype(BF)
    if len(outs) == len(cuts):
        outs[-1][...] = held[:, rows:]


def turn(z_at, got, rows, cuts):
    n_z = len(got)
    outs = [shape((cuts[i + 1] - cuts[i], rows * n_z), BF) for i in range(len(cuts) - 1)]
    if got[0].shape[0] > rows:
        outs.append(shape((n_z, got[0].shape[0] - rows, got[0].shape[1]), BF))
    return pl.pallas_call(
        functools.partial(turn_kernel, n_z, rows, cuts),
        in_specs=[pl.BlockSpec(memory_space=pltpu.SMEM)] + [pl.BlockSpec(memory_space=pltpu.VMEM)] * n_z,
        out_shape=outs,
        scratch_shapes=[pltpu.VMEM((n_z,) + got[0].shape, BF)],
        compiler_params=params(),
        cost_estimate=cost(3),
    )(z_at, *got)


def turn_w_kernel(n_z, at_ref, *refs):
    got, out_got = refs[:n_z], refs[n_z : 2 * n_z]
    w_out, held, out_held = refs[2 * n_z :]
    for k in range(n_z):
        held[at_ref[0] ^ k] = got[k][...]
        out_held[at_ref[0] ^ k] = out_got[k][...]
    columns_part = jnp.concatenate([held[z].astype(F32).T for z in range(n_z)], 1)
    rows = [out_held[z].astype(F32) for z in range(n_z)]
    w_out[...] = jnp.concatenate([columns_part] + rows, 0).astype(BF)


def turn_w(z_at, got, out_got):
    n_z = len(got)
    rows, lanes = got[0].shape
    return pl.pallas_call(
        functools.partial(turn_w_kernel, n_z),
        in_specs=[SMEM] + [pl.BlockSpec(memory_space=pltpu.VMEM)] * (2 * n_z),
        out_shape=shape((lanes + n_z * out_got[0].shape[0], rows * n_z), BF),
        scratch_shapes=[pltpu.VMEM((n_z, rows, lanes), BF), pltpu.VMEM((n_z,) + out_got[0].shape, BF)],
        compiler_params=params(),
        cost_estimate=cost(3),
    )(z_at, *got, *out_got)


def split_kernel(n_z, width, n_in, *refs):
    total = refs[0][...].astype(F32)
    for ref in refs[1:n_in]:
        total = total + ref[...].astype(F32)
    qkv_out, out_out = refs[n_in:]
    model = total.shape[1]
    part = width // n_z
    turned = total[: 3 * width].T
    rows = model // n_z
    bias = total[4 * width : 4 * width + 1]
    for z in range(n_z):
        qkv_out[z] = turned[z * rows : (z + 1) * rows].astype(BF)
        pieces = [total[3 * width + z * part : 3 * width + (z + 1) * part]]
        for i in range(4):
            at = i * width + z * part
            pieces.append(jnp.concatenate([bias[:, at : at + part], jnp.zeros((1, model - part), F32)], 1))
        spare = out_out.shape[1] - part - 4
        if spare:
            pieces.append(jnp.zeros((spare, model), F32))
        out_out[z] = jnp.concatenate(pieces, 0).astype(BF)


def split_parts(values, n_z):
    rows, model = values[0].shape
    width = (rows - 16) // 4
    out_rows = -(-(width // n_z + 4) // 8) * 8
    return pl.pallas_call(
        functools.partial(split_kernel, n_z, width, len(values)),
        out_shape=[shape((n_z, model // n_z, 3 * width), BF), shape((n_z, out_rows, model), BF)],
        compiler_params=params(),
        cost_estimate=cost(3),
    )(*values)


def deal_kernel(n_in, blocks, *refs):
    sums = []
    for i in range(2):
        total = refs[i * n_in][...].astype(F32)
        for ref in refs[i * n_in + 1 : (i + 1) * n_in]:
            total = total + ref[...].astype(F32)
        sums.append(total)
    total = jnp.concatenate(sums, 1)
    rows = total.shape[0] // blocks
    for e in range(blocks):
        refs[2 * n_in][e] = total[e * rows : (e + 1) * rows].astype(BF)


def deal(first, second, blocks):
    rows = first[0].shape[0]
    lanes = first[0].shape[1] + second[0].shape[1]
    return pl.pallas_call(
        functools.partial(deal_kernel, len(first), blocks),
        out_shape=shape((blocks, rows // blocks, lanes), BF),
        compiler_params=params(),
        cost_estimate=cost(3),
    )(*first, *second)


def turn_up_kernel(n_z, at_ref, *refs):
    got, (out, held) = refs[:n_z], refs[n_z:]
    for t in range(n_z):
        total = got[t][0].astype(F32)
        for s in range(1, got[t].shape[0]):
            total = total + got[t][s].astype(F32)
        held[lax.rem(at_ref[0] - t + n_z, n_z)] = total
    turned = jnp.concatenate([held[z].T for z in range(n_z)], 1)
    rows = out.shape[1]
    for z in range(n_z):
        out[z] = turned[z * rows : (z + 1) * rows].astype(BF)


def turn_up(z_at, got):
    n_z = len(got)
    _, ff, model = got[0].shape
    return pl.pallas_call(
        functools.partial(turn_up_kernel, n_z),
        in_specs=[pl.BlockSpec(memory_space=pltpu.SMEM)] + [pl.BlockSpec(memory_space=pltpu.VMEM)] * n_z,
        out_shape=shape((n_z, model // n_z, n_z * ff), BF),
        scratch_shapes=[pltpu.VMEM((n_z, ff, model), F32)],
        compiler_params=params(),
        cost_estimate=cost(3),
    )(z_at, *got)


def columns_kernel(groups, n_in, *refs):
    for out, (source, rows, start, size, count) in zip(refs[n_in:], groups):
        ref = refs[source]
        pieces = []
        for i in range(count):
            for n in range(ref.shape[0]):
                pieces.append(ref[n].astype(F32)[:rows, start + i * size : start + (i + 1) * size])
        out[...] = jnp.concatenate(pieces, 1)


def columns(sources, groups):
    return pl.pallas_call(
        functools.partial(columns_kernel, groups, len(sources)),
        out_shape=[shape((rows, sources[i].shape[0] * size * count), F32) for i, rows, _, size, count in groups],
        compiler_params=params(),
        cost_estimate=cost(3),
    )(*sources)


def mod_columns_kernel(early_ref, late_ref, out):
    shard = out.shape[0]
    pieces = []
    for ref in (early_ref, late_ref):
        for i in range(ref.shape[2] // shard):
            for n in range(ref.shape[0]):
                pieces.append(ref[n].astype(F32)[:shard, i * shard : (i + 1) * shard])
    out[...] = jnp.concatenate(pieces, 1)


def mod_columns(early, late, shard):
    return pl.pallas_call(
        mod_columns_kernel,
        out_shape=[shape((shard, 6 * shard * early.shape[0]), F32)],
        compiler_params=params(),
        cost_estimate=cost(3),
    )(early, late)


def place_kernel(at_ref, *refs):
    out = refs[-1]
    for k, ref in enumerate(refs[:-1]):
        out[at_ref[0] ^ k] = ref[...]


def place(at, got):
    return pl.pallas_call(
        place_kernel,
        in_specs=[pl.BlockSpec(memory_space=pltpu.SMEM)] + [pl.BlockSpec(memory_space=pltpu.VMEM)] * len(got),
        out_shape=shape((len(got),) + got[0].shape, got[0].dtype),
        compiler_params=params(),
        cost_estimate=cost(3),
    )(at, *got)


def attn_fwd_kernel(head_size, h_ref, w_a, w_b, qb_ref, vb_ref, segc_ref, segr_ref, *rest):
    q_out, k_out, v_out, att_out, lse_out = rest[-5:]
    width = qb_ref.shape[-1]
    length = segr_ref.shape[-1]
    model = h_ref.shape[-1]
    h = h_ref[...].reshape(length, model)
    allowed = segc_ref[0] == segr_ref[0]
    scale = head_size ** (-0.5)
    part = q_out.shape[1:]
    for n, w_ref in enumerate((w_a, w_b)):
        qkv = dot_nt(h, w_ref[: 3 * width])
        q = (qkv[:, :width] + qb_ref[n]).astype(BF)
        k = qkv[:, width : 2 * width].astype(BF)
        v = (qkv[:, 2 * width :] + vb_ref[n]).astype(BF)
        q_out[n] = q.reshape(part)
        k_out[n] = k.reshape(part)
        v_out[n] = v.reshape(part)
        pieces = []
        for i in range(width // head_size):
            cut = slice(i * head_size, (i + 1) * head_size)
            score = jnp.where(allowed, dot_nt(k[:, cut], q[:, cut]) * scale, -1e30)
            top = jnp.max(score, 0, keepdims=True)
            prob = jnp.exp(score - top)
            total = jnp.sum(prob, 0, keepdims=True)
            out_t = dot_tn(v[:, cut], prob.astype(BF)) * (1.0 / total)
            pieces.append(out_t.T)
            lse_out[n, 0, i : i + 1, :] = top + jnp.log(total)
        att_out[n] = jnp.concatenate(pieces, -1).astype(BF).reshape(part)


def attn_fwd(hidden, w_a, w_b, query_bias, value_bias, seg_col, seg_row, head_size, wait):
    n_seq, rows, kept_count, model = hidden.shape
    width = query_bias.shape[-1]
    length = n_seq * kept_count
    heads = width // head_size
    token = pl.BlockSpec((n_seq, 1, kept_count, model), lambda r: (0, r, 0, 0))
    part = pl.BlockSpec((2, n_seq, 1, kept_count, width), lambda r: (0, 0, r, 0, 0))
    weight = pl.BlockSpec(w_a.shape, lambda r: (0, 0))
    bias = pl.BlockSpec((2, 1, width), lambda r: (0, 0, 0))
    part_shape = shape((2, n_seq, rows, kept_count, width), BF)
    return pl.pallas_call(
        functools.partial(attn_fwd_kernel, head_size),
        grid=(rows,),
        in_specs=[
            token, weight, weight, bias, bias,
            pl.BlockSpec((1, length, 1), lambda r: (r, 0, 0)),
            pl.BlockSpec((1, 1, length), lambda r: (r, 0, 0)),
        ]
        + [ANY] * len(wait),
        out_specs=[part, part, part, part, pl.BlockSpec((2, 1, heads, length), lambda r: (0, r, 0, 0))],
        out_shape=[part_shape] * 4 + [shape((2, rows, heads, length), F32)],
        compiler_params=params(),
        cost_estimate=cost(12),
    )(hidden, w_a, w_b, query_bias, value_bias, seg_col, seg_row, *wait)


def attn_bwd_kernel(head_size, first, n_wait, h_ref, gb_ref, w_a, w_b, q_ref, k_ref, v_ref, att_ref, lse_ref,
                    bias_ref, segc_ref, segr_ref, *rest):
    g_a, g_b, gh_out, sum_qkv, sum_out, sum_bias = rest[-6:]
    gh_in = None if first else rest[n_wait]
    width = q_ref.shape[-1]
    length = segr_ref.shape[-1]
    model = h_ref.shape[-1]
    row = pl.program_id(0)
    h = h_ref[...].reshape(length, model)
    gb = gb_ref[...].reshape(length, model)
    allowed = segc_ref[0] == segr_ref[0]
    scale = head_size ** (-0.5)
    total = None
    for n, w_ref in enumerate((w_a, w_b)):
        grad_att = dot_nt(gb, w_ref[3 * width :]).astype(BF)
        q = q_ref[n].reshape(length, width)
        k = k_ref[n].reshape(length, width)
        v = v_ref[n].reshape(length, width)
        att = att_ref[n].reshape(length, width)
        gq, gk, gv = [], [], []
        for i in range(width // head_size):
            cut = slice(i * head_size, (i + 1) * head_size)
            score = dot_nt(k[:, cut], q[:, cut]) * scale - lse_ref[n, 0, i : i + 1, :]
            prob = jnp.exp(jnp.where(allowed, score, -1e30))
            grad_prob = dot_nt(v[:, cut], grad_att[:, cut])
            inner = jnp.sum(prob * grad_prob, 0, keepdims=True)
            grad_score = (prob * (grad_prob - inner)).astype(BF)
            gq.append((dot_tn(k[:, cut], grad_score) * scale).T)
            gk.append(dot_nn(grad_score, q[:, cut]) * scale)
            gv.append(dot_nn(prob.astype(BF), grad_att[:, cut]))
        grad_qkv = jnp.concatenate(gq + gk + gv, -1).astype(BF)
        term = dot_nn(grad_qkv, w_ref[: 3 * width])
        total = term if total is None else total + term
        term_qkv = dot_tn(grad_qkv, h)
        term_out = dot_tn(att, gb)
        term_bias = jnp.sum(grad_qkv.astype(F32), 0, keepdims=True)

        @pl.when(row == 0)
        def _():
            sum_qkv[n] = term_qkv
            sum_out[n] = term_out
            sum_bias[n] = term_bias

        @pl.when(row != 0)
        def _():
            sum_qkv[n] += term_qkv
            sum_out[n] += term_out
            sum_bias[n] += term_bias

    if first:
        gh_out[...] = total.reshape(gh_out.shape)
    else:
        gh_out[...] = gh_in[...] + total.reshape(gh_out.shape)

    @pl.when(row == pl.num_programs(0) - 1)
    def _():
        for n, g_ref in enumerate((g_a, g_b)):
            g_ref[: 3 * width] = sum_qkv[n].astype(BF)
            g_ref[3 * width : 4 * width] = sum_out[n].astype(BF)
            biases = jnp.concatenate(
                [sum_bias[n, :, :width], sum_bias[n, :, 2 * width :], bias_ref[n],
                 jnp.zeros((1, model - 4 * width), F32)], -1
            )
            g_ref[4 * width :] = jnp.broadcast_to(biases, (16, model)).astype(BF)


def attn_bwd(hidden, grad_branch, w_a, w_b, saved, bias, seg_col, seg_row, head_size, grad_hidden, wait):
    q, k, v, att, lse = saved
    n_seq, rows, kept_count, model = hidden.shape
    width = q.shape[-1]
    length = n_seq * kept_count
    heads = width // head_size
    first = grad_hidden is None
    token = pl.BlockSpec((n_seq, 1, kept_count, model), lambda r: (0, r, 0, 0))
    part = pl.BlockSpec((2, n_seq, 1, kept_count, width), lambda r: (0, 0, r, 0, 0))
    weight = pl.BlockSpec(w_a.shape, lambda r: (0, 0))
    out = pl.BlockSpec((4 * width + 16, model), lambda r: (0, 0))
    own = [] if first else [grad_hidden]
    return pl.pallas_call(
        functools.partial(attn_bwd_kernel, head_size, first, len(wait)),
        grid=(rows,),
        in_specs=[
            token, token, weight, weight, part, part, part, part,
            pl.BlockSpec((2, 1, heads, length), lambda r: (0, r, 0, 0)),
            pl.BlockSpec((2, 1, 2 * width), lambda r: (0, 0, 0)),
            pl.BlockSpec((1, length, 1), lambda r: (r, 0, 0)),
            pl.BlockSpec((1, 1, length), lambda r: (r, 0, 0)),
        ]
        + [ANY] * len(wait)
        + [token] * len(own),
        out_specs=[out, out, token],
        scratch_shapes=[
            pltpu.VMEM((2, 3 * width, model), F32),
            pltpu.VMEM((2, width, model), F32),
            pltpu.VMEM((2, 1, 3 * width), F32),
        ],
        out_shape=[shape((4 * width + 16, model), BF)] * 2 + [shape(hidden.shape, F32)],
        input_output_aliases={} if first else {12 + len(wait): 2},
        compiler_params=params(),
        cost_estimate=cost(24),
    )(hidden, grad_branch, w_a, w_b, q, k, v, att, lse, bias, seg_col, seg_row, *wait, *own)


def pick_slot(table_ref, ends, seg, index):
    first, last = ends
    low = table_ref[0, first, index : index + 1, :]
    return jnp.where(seg == last, table_ref[0, last, index : index + 1, :], low)


def add_slots(out_ref, ends, seg, values, start):
    first, last = ends

    @pl.when(start)
    def _():
        out_ref[...] = jnp.zeros_like(out_ref)

    @pl.when(first == last)
    def _():
        for index, value in enumerate(values):
            out_ref[0, first, index : index + 1] += jnp.sum(value, 0, keepdims=True)

    @pl.when(first != last)
    def _():
        for index, value in enumerate(values):
            out_ref[0, first, index : index + 1] += jnp.sum(jnp.where(seg == first, value, 0.0), 0, keepdims=True)
            out_ref[0, last, index : index + 1] += jnp.sum(jnp.where(seg == last, value, 0.0), 0, keepdims=True)


def ends_of(ends_ref):
    row, part = pl.program_id(0), pl.program_id(1)
    return ends_ref[0, part, row], ends_ref[1, part, row]


def before_attn_kernel(ends_ref, x_ref, seg_ref, table_ref, out_ref):
    ends, seg = ends_of(ends_ref), seg_ref[0, 0]
    normed, _ = normalize(x_ref[0, 0].astype(F32))
    out_ref[0, 0] = (normed * (1.0 + pick_slot(table_ref, ends, seg, 1)) + pick_slot(table_ref, ends, seg, 0)).astype(BF)


def before_attn(ends, inputs, seg, table):
    n_seq, rows, kept_count, model = inputs.shape
    slots = table.shape[1]
    token = pl.BlockSpec((1, 1, kept_count, model), lambda r, j: (j, r, 0, 0))
    return pl.pallas_call(
        before_attn_kernel,
        grid=(rows, n_seq),
        in_specs=[
            SMEM, token,
            pl.BlockSpec((1, 1, kept_count, 1), lambda r, j: (j, r, 0, 0)),
            pl.BlockSpec((1, slots, 6, model), lambda r, j: (r, 0, 0, 0)),
        ],
        out_specs=token,
        out_shape=shape(inputs.shape, BF),
        compiler_params=params(),
        cost_estimate=cost(5),
    )(ends, inputs, seg, table)


def after_attn_kernel(n_seq, width, out_at, ends_ref, x_ref, seg_ref, table_ref, ob_ref, *rest):
    att_refs, w_refs = rest[:n_seq], rest[n_seq : 3 * n_seq]
    br_out, mid_out, h2_out = rest[-3:]
    kept_count, model = x_ref.shape[2:]
    ends, seg = ends_of(ends_ref), seg_ref[0, 0]
    branch = ob_ref[...]
    for j in range(n_seq):
        for n in range(2):
            w = w_refs[j + n * n_seq][pl.ds(out_at, width)]
            branch = branch + dot_nn(att_refs[j][n].reshape(kept_count, width), w)
    mid = x_ref[0, 0].astype(F32) + pick_slot(table_ref, ends, seg, 2) * branch
    normed, _ = normalize(mid)
    br_out[0, 0] = branch
    mid_out[0, 0] = mid
    h2_out[0, 0] = (normed * (1.0 + pick_slot(table_ref, ends, seg, 4)) + pick_slot(table_ref, ends, seg, 3)).astype(BF)


def after_attn(ends, inputs, seg, table, out_bias, weights, atts):
    n_seq, rows, kept_count, model = inputs.shape
    width = atts[0].shape[-1]
    slots = table.shape[1]
    token = pl.BlockSpec((1, 1, kept_count, model), lambda r, j: (j, r, 0, 0))
    part = pl.BlockSpec((2, 1, 1, kept_count, width), lambda r, j: (0, j, r, 0, 0))
    if width % 16 == 0:
        weight, out_at = pl.BlockSpec((width, model), lambda r, j: (3, 0)), 0
    else:
        weight, out_at = pl.BlockSpec((4 * width, model), lambda r, j: (0, 0)), 3 * width
    return pl.pallas_call(
        functools.partial(after_attn_kernel, n_seq, width, out_at),
        grid=(rows, n_seq),
        in_specs=[
            SMEM, token,
            pl.BlockSpec((1, 1, kept_count, 1), lambda r, j: (j, r, 0, 0)),
            pl.BlockSpec((1, slots, 6, model), lambda r, j: (r, 0, 0, 0)),
            pl.BlockSpec((1, model), lambda r, j: (0, 0)),
        ]
        + [part] * len(atts)
        + [weight] * len(weights),
        out_specs=[token] * 3,
        out_shape=[shape(inputs.shape, F32), shape(inputs.shape, F32), shape(inputs.shape, BF)],
        compiler_params=params(),
        cost_estimate=cost(11),
    )(ends, inputs, seg, table, out_bias, *atts, *weights)


def after_mlp_kernel(ends_ref, mid_ref, mlp_ref, gh_ref, br_ref, ct_ref, seg_ref, table_ref, db_ref, *rest):
    res_out, gm_out, gb_out, sums_out, obias_out = rest[-5:]
    ends, seg = ends_of(ends_ref), seg_ref[0, 0]
    step = pl.program_id(1)
    mid = mid_ref[0, 0]
    branch_mlp = mlp_ref[0, 0] + db_ref[...]
    grad_hidden = gh_ref[0, 0]
    grad_result = ct_ref[0, 0].astype(F32)
    res_out[0, 0] = (mid + pick_slot(table_ref, ends, seg, 5) * branch_mlp).astype(BF)
    normed, inv = normalize(mid)
    grad_mid = grad_result + norm_back(grad_hidden * (1.0 + pick_slot(table_ref, ends, seg, 4)), normed, inv)
    gm_out[0, 0] = grad_mid
    grad_branch = (grad_mid * pick_slot(table_ref, ends, seg, 2)).astype(BF)
    gb_out[0, 0] = grad_branch
    values = [grad_mid * br_ref[0, 0], grad_hidden, grad_hidden * normed, grad_result * branch_mlp]
    add_slots(sums_out, ends, seg, values, step == 0)
    start = jnp.logical_and(step == 0, pl.program_id(0) == 0)
    part = jnp.sum(grad_branch.astype(F32), 0, keepdims=True)
    obias_out[...] = jnp.where(start, 0.0, obias_out[...]) + part


def after_mlp(ends, mid, mlp, grad_hidden, branch, cotangent, seg, table, down_bias, wait):
    n_seq, rows, kept_count, model = mid.shape
    slots = table.shape[1]
    token = pl.BlockSpec((1, 1, kept_count, model), lambda r, j: (j, r, 0, 0))
    vector = pl.BlockSpec((1, model), lambda r, j: (0, 0))
    return pl.pallas_call(
        after_mlp_kernel,
        grid=(rows, n_seq),
        in_specs=[
            SMEM, token, token, token, token, token,
            pl.BlockSpec((1, 1, kept_count, 1), lambda r, j: (j, r, 0, 0)),
            pl.BlockSpec((1, slots, 6, model), lambda r, j: (r, 0, 0, 0)),
            vector,
        ]
        + [ANY] * len(wait),
        out_specs=[
            token, token, token,
            pl.BlockSpec((1, slots, 4, model), lambda r, j: (r, 0, 0, 0)),
            vector,
        ],
        out_shape=[
            shape(mid.shape, BF), shape(mid.shape, F32), shape(mid.shape, BF),
            shape((rows, slots, 4, model), F32), shape((1, model), F32),
        ],
        compiler_params=params(),
        cost_estimate=cost(13),
    )(ends, mid, mlp, grad_hidden, branch, cotangent, seg, table, down_bias, *wait)


def last_kernel(ends_ref, x_ref, gh_ref, gm_ref, seg_ref, table_ref, *rest):
    gx_out, sums_out = rest[-2:]
    ends, seg = ends_of(ends_ref), seg_ref[0, 0]
    grad_hidden = gh_ref[0, 0]
    normed, inv = normalize(x_ref[0, 0].astype(F32))
    back = norm_back(grad_hidden * (1.0 + pick_slot(table_ref, ends, seg, 1)), normed, inv)
    gx_out[0, 0] = (gm_ref[0, 0] + back).astype(BF)
    add_slots(sums_out, ends, seg, [grad_hidden, grad_hidden * normed], pl.program_id(1) == 0)


def last_step(ends, inputs, grad_hidden, grad_mid, seg, table, wait):
    n_seq, rows, kept_count, model = inputs.shape
    slots = table.shape[1]
    token = pl.BlockSpec((1, 1, kept_count, model), lambda r, j: (j, r, 0, 0))
    return pl.pallas_call(
        last_kernel,
        grid=(rows, n_seq),
        in_specs=[
            SMEM, token, token, token,
            pl.BlockSpec((1, 1, kept_count, 1), lambda r, j: (j, r, 0, 0)),
            pl.BlockSpec((1, slots, 6, model), lambda r, j: (r, 0, 0, 0)),
        ]
        + [ANY] * len(wait),
        out_specs=[token, pl.BlockSpec((1, slots, 2, model), lambda r, j: (r, 0, 0, 0))],
        out_shape=[shape(inputs.shape, BF), shape((rows, slots, 2, model), F32)],
        compiler_params=params(),
        cost_estimate=cost(8),
    )(ends, inputs, grad_hidden, grad_mid, seg, table, *wait)


def mlp_kernel(n_up, n_down, first, n_wait, h_ref, gm_ref, ub_ref, *rest):
    up_refs = rest[:n_up]
    down_refs = rest[n_up : n_up + n_down]
    if first:
        mlp_in = gh_in = None
    else:
        mlp_in, gh_in = rest[n_up + n_down + n_wait : n_up + n_down + n_wait + 2]
    mlp_out, gh_out, own_out, other_out, gub_out, up, down, sum_up, sum_down, sum_bias = rest[-10:]
    step = pl.program_id(0)
    model = h_ref.shape[-1]

    @pl.when(step == 0)
    def _():
        for refs, whole in ((up_refs, up), (down_refs, down)):
            at = 0
            for ref in refs:
                block = ref[...].reshape(-1, model)
                whole[at : at + block.shape[0]] = block
                at += block.shape[0]

    h = h_ref[...]
    gm = gm_ref[...]
    pre = dot_nt(h, up[...]) + ub_ref[0]
    square = pre * pre
    tanh_part = jnp.tanh(GELU_C * pre * (1.0 + GELU_A * square))
    half = 0.5 * (1.0 + tanh_part)
    activated = (pre * half).astype(BF)
    slope = half + 0.5 * pre * (1.0 - tanh_part * tanh_part) * GELU_C * (1.0 + 3.0 * GELU_A * square)
    grad_pre = (dot_nt(gm, down[...]) * slope).astype(BF)
    mlp_term = dot_nn(activated, down[...])
    gh_term = dot_nn(grad_pre, up[...])
    mlp_out[...] = mlp_term if first else mlp_in[...] + mlp_term
    gh_out[...] = gh_term if first else gh_in[...] + gh_term
    up_term = dot_tn(grad_pre, h)
    down_term = dot_tn(activated, gm)
    bias_term = jnp.sum(grad_pre.astype(F32), 0, keepdims=True)

    @pl.when(step == 0)
    def _():
        sum_up[...] = up_term
        sum_down[...] = down_term
        sum_bias[...] = bias_term

    @pl.when(step != 0)
    def _():
        sum_up[...] += up_term
        sum_down[...] += down_term
        sum_bias[...] += bias_term

    @pl.when(step == pl.num_programs(0) - 1)
    def _():
        half_rows = sum_up.shape[0] // 2
        own_out[0] = sum_up[:half_rows].astype(BF)
        own_out[1] = sum_down[:half_rows].astype(BF)
        other_out[0] = sum_up[half_rows:].astype(BF)
        other_out[1] = sum_down[half_rows:].astype(BF)
        gub_out[...] = sum_bias[...]


def mlp_step(hidden, grad_mlp, up_bias, ups, downs, sums, wait):
    count, model = hidden.shape
    chunk = min(1024, count)
    width = sum(u.shape[0] * u.shape[1] for u in ups)
    first = sums is None
    own = [] if first else list(sums)
    token = pl.BlockSpec((chunk, model), lambda i: (i, 0))
    weights = [pl.BlockSpec(u.shape, lambda i: (0, 0, 0)) for u in ups + downs]
    grads = pl.BlockSpec((2, width // 2, model), lambda i: (0, 0, 0))
    inputs = 3 + len(ups) + len(downs) + len(wait)
    return pl.pallas_call(
        functools.partial(mlp_kernel, len(ups), len(downs), first, len(wait)),
        grid=(count // chunk,),
        in_specs=[token, token, pl.BlockSpec((1, 1, width), lambda i: (0, 0, 0))]
        + weights
        + [ANY] * len(wait)
        + [token] * len(own),
        out_specs=[token, token, grads, grads, pl.BlockSpec((1, width), lambda i: (0, 0))],
        out_shape=[
            shape((count, model), F32), shape((count, model), F32),
            shape((2, width // 2, model), BF), shape((2, width // 2, model), BF), shape((1, width), F32),
        ],
        scratch_shapes=[
            pltpu.VMEM((width, model), BF), pltpu.VMEM((width, model), BF),
            pltpu.VMEM((width, model), F32), pltpu.VMEM((width, model), F32), pltpu.VMEM((1, width), F32),
        ],
        input_output_aliases={} if first else {inputs: 0, inputs + 1: 1},
        compiler_params=params(),
        cost_estimate=cost(32),
    )(hidden, grad_mlp, up_bias, *ups, *downs, *wait, *own)


def tie(value, *after):
    return lax.optimization_barrier((value,) + after)[0]


def body(
    n_z, n_seq,
    tokens, conditioning, segments, kept, cotangent,
    mod_weight, mod_bias, qkv_weight, query_bias, value_bias, out_weight, out_bias,
    up_weight, up_bias, down_weight, down_bias,
):
    row_count, seq_tokens, model = tokens.shape
    kept_count = kept.shape[1]
    slots = conditioning.shape[1]
    head_size = model // HEADS
    rows = row_count // n_seq
    shard = qkv_weight.shape[0]
    blocks = 2 * n_seq
    devices = n_z * blocks
    width = model // blocks
    part = width // n_z
    flat = n_seq * rows * kept_count
    ff_shard = down_weight.shape[0]
    z_at = lax.axis_index("z")
    core_at = lax.axis_index("core")
    seq_at = lax.axis_index("seq")
    block_at = core_at * n_seq + seq_at
    relative = block_at ^ jnp.arange(blocks)
    z_relative = z_at ^ jnp.arange(n_z)
    seq_relative = seq_at ^ jnp.arange(n_seq)
    core_relative = core_at ^ jnp.arange(2)
    z_ring = (z_at - jnp.arange(n_z)) % n_z
    seq_scalar = seq_at.reshape(1).astype(jnp.int32)
    z_scalar = z_at.reshape(1).astype(jnp.int32)
    mod_shard = 6 * shard

    def over_core(value):
        return lax.ppermute(value, "core", [(0, 1), (1, 0)])

    def over_seq(value, by):
        return lax.ppermute(value, "seq", [(i, i ^ by) for i in range(n_seq)])

    def over_z(value, by):
        return lax.ppermute(value, "z", [(i, i ^ by) for i in range(n_z)])

    def shift_z(value, by):
        return lax.ppermute(value, "z", [(i, (i + by) % n_z) for i in range(n_z)])

    def all_to_all(value):
        return lax.all_to_all(value, EVERY, 0, 0, tiled=True)

    def dense_to_all(value):
        return lax.all_to_all(value, DENSE, 0, 0, tiled=True)

    def to_z(value):
        mine = [lax.dynamic_index_in_dim(value, z_at ^ k, 0, keepdims=False) for k in range(n_z)]
        return [mine[0]] + [over_z(mine[k], k) for k in range(1, n_z)]

    def sum_of(values):
        total = values[0].astype(F32)
        for value in values[1:]:
            total = total + value.astype(F32)
        return total

    def plane(value):
        return [value] + [over_seq(value, j) for j in range(1, n_seq)]

    def seq_to_all(value):
        return lax.all_to_all(value, "seq", 0, 0, tiled=True)

    def gather_seq(value):
        return seq_to_all(jnp.broadcast_to(value[None], (n_seq,) + value.shape))

    def to_rows(value):
        return seq_to_all(value.reshape((n_seq, rows) + value.shape[1:]))

    def from_rows(value):
        return seq_to_all(value).reshape((row_count,) + value.shape[2:])

    first_cols = pack(
        n_z, blocks, qkv_weight, mod_weight, up_weight, (mod_bias, query_bias, value_bias, out_bias, up_bias, down_bias)
    )
    first_got = dense_to_all(first_cols)
    spread_out = []
    for d in range(devices):
        z, c, s = d % n_z, (d // n_z) // n_seq, (d // n_z) % n_seq
        spread_out.append((d, (z * 2 + c) * n_seq + s))
    down_got = plane(tie(down_weight, first_cols))
    out_part = lax.ppermute(tie(out_weight, first_cols), EVERY, spread_out)
    out_got = [out_part] + [over_z(out_part, k) for k in range(1, n_z)]

    places = jnp.arange(seq_tokens, dtype=jnp.int32)
    kept = tie(kept, first_cols)
    hits = kept[:, :, None] == places
    pick = hits.astype(BF)
    kept_here = jnp.any(hits, 1)

    def pick_kept(value):
        return jnp.einsum("rkt,rtd->rkd", pick, value, preferred_element_type=F32).astype(BF)

    def put_kept(value, base):
        spread = jnp.einsum("rkt,rkd->rtd", pick, value, preferred_element_type=F32).astype(BF)
        return jnp.where(kept_here[:, :, None], spread, base)

    picked = pick_kept(tokens)
    picked_ct = pick_kept(cotangent)
    inputs = to_rows(tie(picked, first_got))

    cond_float = conditioning.astype(F32).reshape(row_count * slots, model)
    cond_act = (cond_float / (1.0 + jnp.exp(-cond_float))).astype(BF)
    act_other = over_core(cond_act)
    act_pair = jnp.concatenate([jnp.where(core_at == 0, cond_act, act_other), jnp.where(core_at == 0, act_other, cond_act)])
    act_got = [act_pair] + [over_z(act_pair, k) for k in range(1, n_z)]
    act_all = jnp.take(jnp.stack(act_got), z_relative, axis=0).reshape(-1, model)

    numbers = jnp.arange(slots, dtype=jnp.int32)
    query_seg = jnp.sum(jnp.where(hits, segments[:, None, :], 0), -1)
    kept_hits = jnp.sum((query_seg[:, :, None] == numbers).astype(jnp.int32), 1)
    all_hits = jnp.sum((segments[:, :, None] == numbers).astype(jnp.int32), 1)
    small = jnp.concatenate([query_seg, kept_hits, all_hits - kept_hits], -1)
    small_got = plane(small)
    small = jnp.take(jnp.stack(small_got), seq_relative, axis=0)
    sample_counts = jnp.sum(small[:, :, kept_count:], 0).reshape(row_count, 2, slots).transpose(0, 2, 1)
    seg = lax.dynamic_slice_in_dim(small[:, :, :kept_count], seq_at * rows, rows, 1)
    seg_rows = seg.transpose(1, 0, 2).reshape(rows, 1, n_seq * kept_count)
    seg_cols = seg_rows.reshape(rows, n_seq * kept_count, 1)
    seg_tokens = seg.reshape(n_seq, rows, kept_count, 1)
    ends = jnp.stack([seg[:, :, 0], seg[:, :, -1]])

    qkv_rows, z_cols = unpack(tie(first_got, *act_got[1:], *small_got[1:], *out_got[1:], *down_got[1:], picked), n_z, shard, mod_shard + ff_shard, mod_shard + ff_shard + 4 * shard)
    qkv_got = [qkv_rows] + [over_z(qkv_rows, k) for k in range(1, n_z)]
    w_own = turn_w(z_scalar, qkv_got, out_got)
    z_got = to_z(tie(z_cols, *qkv_got[1:]))
    mod_cols, up_part, bias_got = turn(tie(z_scalar, w_own), z_got, blocks * shard, (0, mod_shard, mod_shard + ff_shard))
    bias_got = bias_got.astype(F32)
    mod_b = bias_got[:, :blocks, :mod_shard].reshape(-1)
    up_b = bias_got[:, :blocks, mod_shard:].reshape(-1)
    query_b, value_b, out_b, down_b = [
        bias_got[:, blocks:, i * shard : (i + 1) * shard].reshape(-1) for i in range(4)
    ]

    mod_part = tie(dot_nt(act_all, mod_cols), inputs).reshape(devices, rows * slots, mod_shard)
    modulation = tie(all_to_all(mod_part), picked_ct).transpose(1, 0, 2).reshape(rows * slots, 6 * model) + mod_b
    table = modulation.reshape(rows, slots, 6, model)

    def token_mod(index):
        value = table[None, :, None, 0, index]
        for slot in range(1, slots):
            value = jnp.where(seg_tokens == slot, table[None, :, None, slot, index], value)
        return value

    hidden_one = before_attn(ends, inputs, seg_tokens, table)

    w_all = plane(w_own)
    w_all = w_all + [over_core(w) for w in w_all]

    down_ring = [place(seq_scalar, down_got)]
    up_ring = [gather_seq(tie(up_part, hidden_one))]
    down_ring.append(shift_z(tie(down_ring[0], *z_got[1:]), 1))
    for t in range(2, n_z):
        if t == 2:
            down_ring.append(shift_z(tie(down_ring[1], hidden_one), 1))
            up_ring.append(shift_z(tie(up_ring[0], down_ring[2]), 1))
        else:
            down_ring.append(shift_z(tie(down_ring[-1], up_ring[-1]), 1))
        up_ring.append(shift_z(tie(up_ring[-1], down_ring[-1]) if t > 2 else up_ring[-1], 1))
    while len(up_ring) < n_z:
        up_ring.append(shift_z(up_ring[-1], 1))
    down_other = [over_core(value) for value in down_ring]
    up_other = [over_core(value) for value in up_ring]

    def by_block(value):
        return jnp.take(value.reshape(blocks, 1, width), relative, axis=0)

    query_b, value_b = by_block(query_b), by_block(value_b)
    up_b = jnp.take(up_b.reshape(n_z, 2, n_seq * ff_shard), core_relative, axis=1)
    up_b = jnp.take(up_b, z_ring, axis=0).reshape(n_z, 1, blocks * ff_shard)

    def pair(value, j):
        return jnp.stack([value[j], value[j + n_seq]])

    saved = []
    for j in range(n_seq):
        saved.append(attn_fwd(
            hidden_one, w_all[j], w_all[j + n_seq], pair(query_b, j), pair(value_b, j), seg_cols, seg_rows, head_size, [],
        ))
    branch_attn, mid, hidden_two = after_attn(
        ends, inputs, seg_tokens, table, out_b.reshape(1, -1), w_all, [s[3] for s in saved],
    )
    grad_result = to_rows(tie(picked_ct, up_ring[0]))
    grad_mlp = (grad_result.astype(F32) * token_mod(5)).astype(BF)
    grad_down_bias = jnp.sum(grad_mlp.astype(F32), (0, 1, 2))

    order = list(range(n_z))
    hidden_flat = hidden_two.reshape(flat, model)
    grad_flat = grad_mlp.reshape(flat, model)
    sums = None
    cores, sends, planes, down_sums, grad_up_bias = [], [], [], {}, {}
    ring = []
    for at, t in enumerate(order):
        ups = [up_ring[t], up_other[t]]
        downs = [down_ring[t], down_other[t]]
        if ff_shard % 16:
            ups = [jnp.concatenate([u.reshape(-1, model) for u in ups])[None]]
            downs = [jnp.concatenate([d.reshape(-1, model) for d in downs])[None]]
        wait = []
        if at >= 2:
            wait.extend(sends[at - 2])
        if at >= 3:
            wait.append(planes[at - 3])
        mlp_sum, gh_sum, own, other, grad_up_bias[t] = mlp_step(
            hidden_flat, grad_flat, up_b[t : t + 1], ups, downs, sums, wait
        )
        sums = (mlp_sum, gh_sum)
        cores.append(over_core(other))
        both = (own.astype(F32) + cores[at].astype(F32)).reshape(2, n_seq, ff_shard, model)
        sends.append([both[0].astype(BF)])
        planes.append(seq_to_all(sends[at][0]))
        down_sums[t] = both[1]
        if t and len(ring) == t - 1:
            value = both[1] if t == 1 else both[1] + ring[-1].astype(F32)
            sends[at].append(value.astype(BF))
            ring.append(shift_z(sends[at][1], 1))

    last = n_z - 1
    res, grad_mid, grad_branch, sums_late, grad_out_bias = after_mlp(
        ends, mid, sums[0].reshape(mid.shape), sums[1].reshape(mid.shape), branch_attn, grad_result, seg_tokens, table,
        down_b.reshape(1, -1), sends[last - 1] + [planes[last - 2]],
    )

    def natural_block(value):
        return by_block(value.reshape(-1))

    late_bias = jnp.concatenate([natural_block(grad_out_bias), natural_block(grad_down_bias)], -1)
    late = sums_late.reshape(rows * slots, 4, devices, shard).transpose(2, 0, 1, 3).reshape(devices, rows * slots, -1)
    late = late.astype(BF)
    waits = sends[last] + [planes[last - 1]]
    grad_hidden = None
    w_cores, w_values, w_planes = [], [], []
    for at, j in enumerate([n_seq - 1] + list(range(1, n_seq - 1)) + [0]):
        g_own, g_other, grad_hidden = attn_bwd(
            hidden_one, grad_branch, w_all[j], w_all[j + n_seq], saved[j],
            pair(late_bias, j), seg_cols, seg_rows, head_size, grad_hidden, waits,
        )
        waits = []
        if at == 0:
            waits = [planes[last]]
            late = all_to_all(tie(late, g_own)).reshape(-1, 4 * shard)
            res = tie(res, g_own)
            res_mine = [lax.dynamic_index_in_dim(res, seq_at ^ k, 0, keepdims=False) for k in range(n_seq)]
            res_got = [res_mine[0]] + [over_seq(res_mine[k], k) for k in range(1, n_seq)]
            down_last = (down_sums[0] + ring[-1].astype(F32)).astype(BF)
        elif at == 1:
            late_mod = dot_tn(act_all, tie(late, g_own)).astype(BF).reshape(devices, shard, 4 * shard)
            natural = jnp.stack([grad_up_bias[t] for t in range(n_z)]).reshape(n_z, 2, n_seq * ff_shard)
            natural = jnp.take(jnp.take(natural, core_relative, axis=1), z_ring, axis=0).reshape(devices, 1, ff_shard)
            late_got = all_to_all(jnp.concatenate([late_mod, natural.astype(BF)], 1))
            up_bias_grad = jnp.sum(late_got[:, shard].astype(F32), 0)
            up_turned = turn_up(z_scalar, [planes[order.index(t)] for t in range(n_z)])
            up_parts = to_z(up_turned)
            waits = [ring[-1], late, up_turned] + res_got[1:]
        elif at == 2:
            waits = [late_got]
            down_parts = seq_to_all(tie(down_last, g_own))
            down_grad = jnp.sum(down_parts.astype(F32), 0)
        elif at == 3:
            waits = [down_parts] + up_parts[1:]
        w_cores.append(over_core(g_other))
        w_values.append((g_own.astype(F32) + w_cores[at].astype(F32)).astype(BF))
        w_planes.append(over_seq(w_values[at], j) if j else w_values[at])
        if at >= 1:
            waits.append(w_values[at - 1])
        if at == n_seq - 2:
            waits.append(w_values[at])

    grad_x, sums_early = last_step(ends, inputs, grad_hidden, grad_mid, seg_tokens, table, waits)
    def in_place(got):
        return place(seq_scalar, got).reshape((row_count,) + got[0].shape[1:])

    res_got[0] = tie(res_got[0], grad_x)
    output = put_kept(in_place(res_got), tokens)

    qkv_parts, out_parts = split_parts(w_planes, n_z)
    qkv_parts = to_z(qkv_parts)
    out_parts = to_z(out_parts)
    back_out = lax.ppermute(sum_of(out_parts).astype(BF), EVERY, [(t, d) for d, t in spread_out]).astype(F32)
    out_grad = back_out[:part]
    small_grads = back_out[part : part + 4, :part]

    early = sums_early.reshape(rows * slots, 2, devices, shard).transpose(2, 0, 1, 3).reshape(devices, rows * slots, -1)
    early = all_to_all(early.astype(BF)).reshape(-1, 2 * shard)
    grad_got = from_rows(tie(grad_x, early))
    tokens_grad = put_kept(grad_got, cotangent)
    early_mod = dot_tn(act_all, early).astype(BF).reshape(devices, shard, 2 * shard)
    mod_sums = jnp.concatenate([jnp.sum(sums_early, (0, 1)), jnp.sum(sums_late, (0, 1))]).reshape(devices, 6 * shard)
    mod_sums = mod_sums.astype(BF).reshape(devices, 3, 2 * shard)
    mod_got = all_to_all(jnp.concatenate([tie(early_mod, grad_got), mod_sums], 1))
    mod_bias_grad = jnp.sum(mod_got[:, shard:].reshape(devices, -1).astype(F32), 0)
    dense_got = dense_to_all(deal(qkv_parts, up_parts, blocks))
    qkv_grad, up_grad = columns(
        [dense_got], [(0, shard, 0, width, 3), (0, shard, 3 * width, ff_shard, n_z)]
    )
    (mod_grad,) = mod_columns(mod_got, late_got, shard)
    return (
        output, tokens_grad, mod_grad, mod_bias_grad, qkv_grad, small_grads[0], small_grads[1],
        out_grad, small_grads[2], up_grad, up_bias_grad, down_grad, small_grads[3], sample_counts,
    )


def solution(mesh):
    n_batch, n_seq = mesh.shape["batch"], mesh.shape["seq"]
    split = Mesh(mesh.devices.reshape(n_batch // 2, 2, n_seq), ("z", "core", "seq"))
    batch = ("z", "core")
    both = ("z", "core", "seq")
    row_split = P(batch, "seq", None)
    matrix = P(both, None)
    vector = P(both)
    return jax.shard_map(
        functools.partial(body, n_batch // 2, n_seq),
        mesh=split,
        in_specs=(
            row_split, P(batch, None, None), P(batch, "seq"), P(batch, "seq"), row_split,
            matrix, vector, matrix, vector, vector, matrix, vector, matrix, vector, matrix, vector,
        ),
        out_specs=(
            row_split, row_split, matrix, vector, matrix, vector, vector,
            matrix, vector, matrix, vector, matrix, vector, P(batch, None, None),
        ),
        check_vma=False,
    )
```
